32 devices in a mesh: ox: 4 (over y, core), oy: 8 (over z, x).
Axes of the slice: x: 2, y: 2, z: 4, core: 2. Of those that a mesh axis runs over, the one named last changes fastest.
Arguments:
- slip_rate: bfloat16 [4, 1024], P(None, ('ox', 'oy')), may hold values from -6 to 6
- green_kernel: bfloat16 [1024, 9, 8192], P(('ox', 'oy')), may hold values from -1 to 1
- intersection: int32 [32, 9], P(('ox', 'oy')), may hold values 0 or 1
- wet_mask: int32 [1024, 4096], P('ox', 'oy'), may hold values 0 or 1
- column_height: float32 [1024, 4096], P('ox', 'oy'), may hold values from 3 to 5
- east_flow: float32 [1024, 4096], P('ox', 'oy'), may hold values from -3 to 3
- north_flow: float32 [1024, 4096], P('ox', 'oy'), may hold values from -3 to 3
Outputs:
- height_out: float32 [1024, 4096], P('ox', 'oy')
- east_out: float32 [1024, 4096], P('ox', 'oy')
- north_out: float32 [1024, 4096], P('ox', 'oy')
The draws below stay inside these ranges and needn't reach their ends.
All inputs are finite; a program needn't handle non-finite values. No bound on the sum of `intersection` or of `wet_mask` on one device may be relied on, other than what follows from the above.
Results may differ from the reference program's by a relative error of at most 0.0003.
Values sent between devices are 32-bit elements; how exact they have to be, the bound alone decides.
A program may use at most 64 MiB of HBM per device.

```python
import jax
import jax.numpy as jnp
from jax import lax

F_DEV = 32
STEPS = 4
COARSE = 4
NX = 1024
NY = 4096
BLOCKS = 32
FAULTS = 1024
UX = 64
UY = 128
UP = 8192
N_OX = 4
N_OY = 8


def plant(entries, rng, low, high):
    longest = entries.shape.index(max(entries.shape))
    spots = []
    for shift in (0, 1):
        where = [jax.random.randint(jax.random.fold_in(rng, axis), (), 0, length) for axis, length in enumerate(entries.shape)]
        where[longest] = (where[longest] + shift) % entries.shape[longest]
        spots.append(tuple(where))
    return entries.at[spots[0]].set(low).at[spots[1]].set(high)


def levels(rng, shape, shards, low, top_value):
    def one(position, shards_of):
        steps = jax.random.uniform(jax.random.fold_in(jax.random.fold_in(rng, 6), position), (shards_of,), jnp.float32, low / len(shards), top_value / len(shards))
        return jnp.repeat(jnp.exp(steps), shape[position] // shards_of).reshape((-1,) + (1,) * (len(shape) - position - 1))

    factor_of = one(*shards[0])
    for cut in shards[1:]:
        factor_of = factor_of * one(*cut)
    return factor_of


def bell_draw(rng, shape, width, bound, split=(), held_as=jnp.bfloat16):
    array = jax.random.normal(rng, shape, jnp.float32) * width
    if len(split) > 0:
        array = levels(rng, shape, split, -0.22, 0.18) * array
    return jnp.clip(array, min=-bound, max=bound).astype(held_as)


def setup_inputs(seed: int = 0) -> dict:
    key_list = jax.random.split(jax.random.key(seed), 8)
    return {
        "slip_rate": bell_draw(key_list[0], (STEPS, FAULTS), 1.0, 6.0, ((1, 32),)),
        "green_kernel": bell_draw(key_list[1], (FAULTS, 9, UP), F_DEV ** -0.5, 1.0, ((0, 32),)),
        "intersection": plant((jax.random.randint(key_list[2], (BLOCKS, 9), 0, 3) < 2).astype(jnp.int32), jax.random.fold_in(key_list[2], 1), 0, 1),
        "wet_mask": plant((jax.random.randint(key_list[3], (NX, NY), 0, 10) < 9).astype(jnp.int32), jax.random.fold_in(key_list[3], 1), 0, 1),
        "column_height": jnp.clip(3.0 + 2.0 * jax.random.uniform(key_list[4], (NX, NY), jnp.float32) ** levels(key_list[4], (NX, NY), ((0, 4), (1, 8)), -0.2, 0.2), 3.0, 5.0),
        "east_flow": bell_draw(key_list[5], (NX, NY), 0.5, 3.0, ((0, 4), (1, 8)), jnp.float32),
        "north_flow": bell_draw(key_list[6], (NX, NY), 0.5, 3.0, ((0, 4), (1, 8)), jnp.float32),
    }


gravity = 1.0
ratio = 0.2
source = 0.05


def lax_friedrichs(extended):
    height = extended[0]
    east = extended[1]
    north = extended[2]
    flux_x = jnp.stack([east, east * east / height + 0.5 * gravity * height * height, east * north / height])
    flux_y = jnp.stack([north, east * north / height, north * north / height + 0.5 * gravity * height * height])
    average = 0.25 * (extended[:, 2:, 1:-1] + extended[:, :-2, 1:-1] + extended[:, 1:-1, 2:] + extended[:, 1:-1, :-2])
    average = average - 0.5 * ratio * (flux_x[:, 2:, 1:-1] - flux_x[:, :-2, 1:-1])
    return average - 0.5 * ratio * (flux_y[:, 1:-1, 2:] - flux_y[:, 1:-1, :-2])


def reference(slip_rate, green_kernel, intersection, wet_mask, column_height, east_flow, north_flow):
    slips = slip_rate.reshape(STEPS, BLOCKS, F_DEV).transpose(1, 0, 2)
    kernels = green_kernel.reshape(BLOCKS, F_DEV, 9 * UP)

    def one_block(pieces):
        slip_block, kernel_block, cover = pieces
        term = jnp.dot(slip_block, kernel_block, preferred_element_type=jnp.float32).reshape(STEPS, 9, UP)
        return term * cover.astype(jnp.float32)[None, :, None]

    partial_value = lax.map(one_block, (slips, kernels, intersection))
    partial_value = partial_value.reshape(N_OX, N_OY, STEPS, 3, 3, UX, UY)
    coarse = jnp.zeros((N_OX, N_OY, STEPS, UX, UY), jnp.float32)
    for row_off in range(3):
        for col_off in range(3):
            padded = jnp.pad(partial_value[:, :, :, row_off, col_off], ((1, 1), (1, 1), (0, 0), (0, 0), (0, 0)))
            coarse = coarse + padded[2 - row_off:2 - row_off + N_OX, 2 - col_off:2 - col_off + N_OY]
    coarse = coarse.transpose(2, 0, 3, 1, 4).reshape(STEPS, NX // COARSE, NY // COARSE)
    wet = wet_mask.astype(jnp.float32)
    state = jnp.stack([column_height, east_flow, north_flow])
    for section in range(STEPS):
        extended = jnp.pad(state, ((0, 0), (1, 1), (1, 1)), mode="edge")
        updated = lax_friedrichs(extended)
        fine = jnp.repeat(jnp.repeat(coarse[section], COARSE, axis=0), COARSE, axis=1)
        state = jnp.stack([updated[0] + source * fine, updated[1] * wet, updated[2] * wet])
    return state[0], state[1], state[2]
```

```python
import functools

import jax
import jax.numpy as jnp
from jax import lax
from jax.experimental import pallas as pl
from jax.experimental.pallas import tpu as pltpu
from jax.sharding import PartitionSpec as P

COARSE = 4
STRIP = 8
LANES = 128
PAD = 16

gravity = 1.0
ratio = 0.2
source = 0.05

MESH = pl.DeviceIdType.MESH
f32 = jnp.float32
bf16 = jnp.bfloat16


def iota(shape, dim):
    return lax.broadcasted_iota(jnp.int32, shape, dim)


def weights(slip_ref, cover_ref, steps, faults, a):
    rows = -(-3 * steps // PAD) * PAD
    wide = 3 * faults
    pick_step = (iota((rows, steps), 0) // 3 == iota((rows, steps), 1)).astype(bf16)
    pick_fault = (iota((faults, wide), 1) % faults == iota((faults, wide), 0)).astype(bf16)
    slips = jnp.dot(pick_step, slip_ref[...], preferred_element_type=f32).astype(bf16)
    slips = jnp.dot(slips, pick_fault, preferred_element_type=f32)
    slot = iota((rows, wide), 0) % 3
    cover = jnp.zeros((rows, wide), f32)
    for b in range(3):
        cover = jnp.where(slot == b, cover_ref[0, 3 * a + b].astype(f32), cover)
    return jnp.where(slot == iota((rows, wide), 1) // faults, slips * cover, 0.0).astype(bf16)


def flux_terms(h, m, n):
    inv = 1.0 / h
    u = m * inv
    v = n * inv
    pressure = 0.5 * gravity * h * h
    cross = m * v
    half = 0.5 * ratio
    fx = (half * m, half * (m * u + pressure), half * cross)
    fy = (half * n, half * cross, half * (n * v + pressure))
    quarter = (0.25 * h, 0.25 * m, 0.25 * n)
    return quarter, fx, fy


def kernel(
    n_ox, n_oy,
    slip_ref, green_ref, cover_ref, wet_hbm, h_hbm, m_hbm, n_hbm,
    h_out, m_out, n_out,
    green, part, state, wet, fine, spread, cols, halo_cols,
    route_x, summed, route_y, row_out, row_in, col_out, col_in, halo_rows,
    green_sem, load_sem, rx_send, rx_recv, ry_send, ry_recv, row_send, row_recv, col_send, col_recv,
):
    steps, faults = slip_ref.shape
    n_rows, n_cols = wet.shape
    up_rows, up_cols = n_rows // COARSE, n_cols // COARSE
    i, j = lax.axis_index("ox"), lax.axis_index("oy")
    near = (
        (i > 0, (i - 1, j)),
        (i < n_ox - 1, (i + 1, j)),
        (j > 0, (i, j - 1)),
        (j < n_oy - 1, (i, j + 1)),
    )

    loads = []
    for q, (src, dst) in enumerate((
        (h_hbm, state.at[0, 0, pl.ds(STRIP, n_rows)]),
        (m_hbm, state.at[0, 1, pl.ds(STRIP, n_rows)]),
        (n_hbm, state.at[0, 2, pl.ds(STRIP, n_rows)]),
        (wet_hbm, wet),
    )):
        loads.append(pltpu.make_async_copy(src, dst, load_sem.at[q]))
    for copy in loads:
        copy.start()
    chunks = green_sem.shape[1]
    width = green.shape[2] // chunks
    greens = {}
    for a in (2, 0, 1):
        for q in range(chunks):
            where = (pl.ds(3 * a, 3), slice(None), pl.ds(q * width, width))
            greens[a, q] = pltpu.make_async_copy(green_ref.at[where], green.at[where], green_sem.at[a, q])
            greens[a, q].start()

    barrier = pltpu.get_barrier_semaphore()
    for there, device in near:
        @pl.when(there)
        def _():
            pl.semaphore_signal(barrier, inc=1, device_id=device, device_id_type=MESH)

    zero_x = jnp.zeros(route_x.shape[2:], f32)
    zero_y = jnp.zeros(route_y.shape[2:], f32)
    for d in range(2):
        @pl.when(jnp.logical_not(near[d][0]))
        def _():
            for s in range(steps):
                route_x[s, d] = zero_x

        @pl.when(jnp.logical_not(near[2 + d][0]))
        def _():
            for s in range(steps):
                route_y[s, d] = zero_y

    coarse_of = iota((2 * up_cols, n_cols), 1) // COARSE
    spread[...] = (coarse_of == iota((2 * up_cols, n_cols), 0) % up_cols).astype(bf16)
    halo_cols[...] = jnp.zeros(halo_cols.shape, f32)
    lhs = [weights(slip_ref, cover_ref, steps, faults, a) for a in range(3)]

    pl.semaphore_wait(barrier, sum(there.astype(jnp.int32) for there, _ in near))

    def remote(src, dst, send, recv, d):
        return pltpu.make_async_remote_copy(
            src_ref=src, dst_ref=dst, send_sem=send, recv_sem=recv, device_id=near[d][1], device_id_type=MESH
        )

    def when_each(copies, what):
        for d, copy in copies:
            @pl.when(near[d ^ 1 if what == "wait_recv" else d][0])
            def _():
                getattr(copy, what)()

    def route_x_copies(s, sides=(0, 1)):
        rows = 3 * up_rows
        return [
            (d, remote(part.at[2 * d, pl.ds(s * rows, rows)], route_x.at[s, 1 - d], rx_send.at[s, d], rx_recv.at[s, 1 - d], d))
            for d in sides
        ]

    def route_y_copies(s):
        return [
            (2 + d, remote(summed.at[s, d], route_y.at[s, 1 - d], ry_send.at[s, d], ry_recv.at[s, 1 - d], 2 + d))
            for d in range(2)
        ]

    def row_copies(s):
        return [(d, remote(row_out.at[s, d], row_in.at[s, 1 - d], row_send.at[s, d], row_recv.at[s, 1 - d], d)) for d in range(2)]

    def col_copies(s):
        return [
            (2 + d, remote(col_out.at[s], col_in.at[s, 1 - d], col_send.at[s, d], col_recv.at[s, 1 - d], 2 + d))
            for d in range(2)
        ]

    lane = iota((STRIP, LANES), 1)
    first_lane = lane == 0
    last_lane = lane == LANES - 1
    row8 = iota((STRIP, n_cols), 0)

    def edge_columns(fields):
        packed = jnp.zeros((STRIP, LANES), f32)
        for c in range(3):
            first = fields[c][:, :LANES]
            last = fields[c][:, n_cols - LANES:]
            packed = jnp.where(lane == c, first if c == 0 else pltpu.roll(first, c, 1), packed)
            packed = jnp.where(lane == 3 + c, pltpu.roll(last, 4 + c, 1), packed)
        return packed

    def send_edges(s, buf):
        col_out[s] = jnp.transpose(cols[...])[:STRIP]
        for c in range(3):
            row_out[s, 0, pl.ds(c, 1)] = state[buf, c, pl.ds(STRIP, 1)]
            row_out[s, 1, pl.ds(c, 1)] = state[buf, c, pl.ds(STRIP + n_rows - 1, 1)]
        when_each(row_copies(s), "start")
        when_each(col_copies(s), "start")

    for copy in loads:
        copy.wait()

    def pack(k, carry):
        base = pl.multiple_of(k * STRIP, STRIP)
        cols[pl.ds(base, STRIP)] = edge_columns([state[0, c, pl.ds(base + STRIP, STRIP)] for c in range(3)])
        return carry

    lax.fori_loop(0, n_rows // STRIP, pack, 0)
    row_out[...] = jnp.zeros(row_out.shape, f32)
    send_edges(0, 0)

    for a in (2, 0, 1):
        for q in range(chunks):
            greens[a, q].wait()
            block = green[pl.ds(3 * a, 3), :, pl.ds(q * width, width)].reshape(3 * faults, width)
            out = jnp.dot(lhs[a], block, preferred_element_type=f32)
            for p in range(width // up_cols):
                row = q * (width // up_cols) + p
                part[a, pl.ds(row, out.shape[0], stride=up_rows), :] = out[:, p * up_cols:(p + 1) * up_cols]
        if a != 1:
            for s in range(steps):
                when_each(route_x_copies(s, (a // 2,)), "start")

    for s in range(steps):
        when_each(route_x_copies(s), "wait_recv")
        mine = part[1, pl.ds(s * 3 * up_rows, 3 * up_rows), :]
        total = mine + route_x[s, 0] + route_x[s, 1]
        summed[s, 0] = total[:up_rows]
        summed[s, 1] = total[2 * up_rows:]
        summed[s, 2] = total[up_rows:2 * up_rows]
        when_each(route_y_copies(s), "start")

    def receive_edges(s, buf):
        when_each(row_copies(s), "wait_recv")
        when_each(col_copies(s), "wait_recv")
        for d in range(2):
            halo_at = (STRIP - 1, STRIP + n_rows)[d]
            own = (STRIP, STRIP + n_rows - 1)[d]

            @pl.when(near[d][0])
            def _():
                for c in range(3):
                    state[buf, c, pl.ds(halo_at, 1)] = row_in[s, d, pl.ds(c, 1)]

            @pl.when(jnp.logical_not(near[d][0]))
            def _():
                for c in range(3):
                    state[buf, c, pl.ds(halo_at, 1)] = state[buf, c, pl.ds(own, 1)]

        @pl.when(near[3][0])
        def _():
            halo_rows[pl.ds(0, 3)] = col_in[s, 1, pl.ds(0, 3)]

        @pl.when(jnp.logical_not(near[3][0]))
        def _():
            halo_rows[pl.ds(0, 3)] = col_out[s, pl.ds(3, 3)]

        @pl.when(near[2][0])
        def _():
            halo_rows[pl.ds(3, 3)] = col_in[s, 0, pl.ds(3, 3)]

        @pl.when(jnp.logical_not(near[2][0]))
        def _():
            halo_rows[pl.ds(3, 3)] = col_out[s, pl.ds(0, 3)]

        right, _, right_y = flux_terms(*(halo_rows[pl.ds(c, 1)] for c in range(3)))
        left, _, left_y = flux_terms(*(halo_rows[pl.ds(3 + c, 1)] for c in range(3)))
        for c in range(3):
            halo_cols[pl.ds(c, 1), :n_rows] = right[c] - right_y[c]
            halo_cols[pl.ds(3 + c, 1), :n_rows] = left[c] + left_y[c]
        cols[...] = jnp.transpose(halo_cols[...])

    def shifted_pair(c, plus, minus, edge):
        n_blocks = n_cols // LANES
        ups, downs = [], []
        for b in range(n_blocks):
            ups.append(pltpu.roll(plus[:, b * LANES:(b + 1) * LANES], LANES - 1, 1))
            downs.append(pltpu.roll(minus[:, b * LANES:(b + 1) * LANES], 1, 1))
        result = []
        for b in range(n_blocks):
            after = ups[b + 1] if b < n_blocks - 1 else edge[:, c:c + 1]
            before = downs[b - 1] if b > 0 else edge[:, 3 + c:4 + c]
            result.append(jnp.where(last_lane, after, ups[b]) + jnp.where(first_lane, before, downs[b]))
        return jnp.concatenate(result, axis=1)

    def strip_terms(buf, k):
        base = pl.multiple_of(k * STRIP, STRIP)
        quarter, fx, fy = flux_terms(*(state[buf, c, pl.ds(base, STRIP)] for c in range(3)))
        up = [pltpu.roll(quarter[c] - fx[c], STRIP - 1, 0) for c in range(3)]
        down = [pltpu.roll(quarter[c] + fx[c], 1, 0) for c in range(3)]
        return quarter, fy, up, down

    def across(k, quarter, fy):
        edge = cols[pl.ds(pl.multiple_of((k - 1) * STRIP, STRIP), STRIP)]
        return [shifted_pair(c, quarter[c] - fy[c], quarter[c] + fy[c], edge) for c in range(3)]

    def step(s, buf):
        last = s == steps - 1
        n_strips = n_rows // STRIP

        def finish(k, acc, up, next_up):
            base = pl.multiple_of((k - 1) * STRIP, STRIP)
            dry = wet[pl.ds(base, STRIP)].astype(f32)
            values = [acc[c] + jnp.where(row8 == STRIP - 1, next_up[c], up[c]) for c in range(3)]
            lift = jnp.concatenate([fine[b, pl.ds(base, STRIP)] for b in range(n_cols // LANES)], axis=1)
            values = [values[0] + lift, values[1] * dry, values[2] * dry]
            for c in range(3):
                if last:
                    (h_out, m_out, n_out)[c][pl.ds(base, STRIP)] = values[c]
                else:
                    state[1 - buf, c, pl.ds(base + STRIP, STRIP)] = values[c]
            if not last:
                cols[pl.ds(base, STRIP)] = edge_columns(values)

        def start(k, down_before):
            quarter, fy, up, down = strip_terms(buf, k)
            sides = across(k, quarter, fy)
            acc = [sides[c] + jnp.where(row8 == 0, down_before[c], down[c]) for c in range(3)]
            return acc, up, down

        def body(k, carry):
            acc, up, down = carry
            new = start(k, down)
            finish(k - 1, acc, up, new[1])
            return new

        _, _, _, down = strip_terms(buf, 0)
        carry = start(1, down)
        acc, up, down = lax.fori_loop(2, n_strips + 1, body, carry)
        _, _, next_up, _ = strip_terms(buf, n_strips + 1)
        finish(n_strips, acc, up, next_up)

    for s in range(steps):
        buf = s % 2
        when_each(route_y_copies(s), "wait_recv")
        lift = source * (summed[s, 2] + route_y[s, 0] + route_y[s, 1])
        high = lift.astype(bf16)
        low = (lift - high.astype(f32)).astype(bf16)
        wide = jnp.dot(jnp.concatenate([high, low], axis=1), spread[...], preferred_element_type=f32)
        for b in range(n_cols // LANES):
            for t in range(COARSE):
                fine[b, pl.ds(t, up_rows, stride=COARSE), :] = wide[:, b * LANES:(b + 1) * LANES]
        receive_edges(s, buf)
        step(s, buf)
        if s < steps - 1:
            send_edges(s + 1, 1 - buf)

    for s in range(steps):
        when_each(route_x_copies(s), "wait_send")
        when_each(route_y_copies(s), "wait_send")
        when_each(row_copies(s), "wait_send")
        when_each(col_copies(s), "wait_send")


def shards(n_ox, n_oy, slip_rate, green_kernel, intersection, wet_mask, column_height, east_flow, north_flow):
    steps, faults = slip_rate.shape
    rows, cols = column_height.shape
    up_rows, up_cols = rows // COARSE, cols // COARSE
    part_rows = -(-3 * steps // PAD) * PAD * up_rows
    chunks = 4
    anywhere = pl.BlockSpec(memory_space=pl.ANY)
    vmem = pl.BlockSpec(memory_space=pltpu.VMEM)
    dma = pltpu.SemaphoreType.DMA
    return pl.pallas_call(
        functools.partial(kernel, n_ox, n_oy),
        out_shape=[jax.ShapeDtypeStruct((rows, cols), f32)] * 3,
        in_specs=[vmem, anywhere, pl.BlockSpec(memory_space=pltpu.SMEM)] + [anywhere] * 4,
        out_specs=[vmem] * 3,
        scratch_shapes=[
            pltpu.VMEM((9, faults, green_kernel.shape[2]), bf16),
            pltpu.VMEM((3, part_rows, up_cols), f32),
            pltpu.VMEM((2, 3, rows + 2 * STRIP, cols), f32),
            pltpu.VMEM((rows, cols), jnp.int32),
            pltpu.VMEM((cols // LANES, rows, LANES), f32),
            pltpu.VMEM((2 * up_cols, cols), bf16),
            pltpu.VMEM((rows, LANES), f32),
            pltpu.VMEM((LANES, rows), f32),
            pltpu.VMEM((steps, 2, 3 * up_rows, up_cols), f32),
            pltpu.VMEM((steps, 3, up_rows, up_cols), f32),
            pltpu.VMEM((steps, 2, up_rows, up_cols), f32),
            pltpu.VMEM((steps, 2, STRIP, cols), f32),
            pltpu.VMEM((steps, 2, STRIP, cols), f32),
            pltpu.VMEM((steps, STRIP, rows), f32),
            pltpu.VMEM((steps, 2, STRIP, rows), f32),
            pltpu.VMEM((STRIP, rows), f32),
            dma((3, chunks)),
            dma((4,)),
        ] + [dma((steps, 2))] * 8,
        compiler_params=pltpu.CompilerParams(
            collective_id=0, has_side_effects=True, vmem_limit_bytes=60 * 1024 * 1024
        ),
        cost_estimate=pl.CostEstimate(flops=400_000_000, bytes_accessed=16_000_000, transcendentals=0),
    )(slip_rate, green_kernel.transpose(1, 0, 2), intersection, wet_mask, column_height, east_flow, north_flow)


def solution(mesh):
    return jax.shard_map(
        functools.partial(shards, mesh.shape["ox"], mesh.shape["oy"]),
        mesh=mesh,
        in_specs=(
            P(None, ("ox", "oy")),
            P(("ox", "oy"), None, None),
            P(("ox", "oy"), None),
            P("ox", "oy"),
            P("ox", "oy"),
            P("ox", "oy"),
            P("ox", "oy"),
        ),
        out_specs=(P("ox", "oy"), P("ox", "oy"), P("ox", "oy")),
        check_vma=False,
    )
```

```python
import functools

import jax
import jax.numpy as jnp
from jax import lax
from jax.experimental import pallas as pl
from jax.experimental.pallas import tpu as pltpu
from jax.sharding import PartitionSpec as P

COARSE = 4
STRIP = 8
LANES = 128
PAD = 16
GROUP = 4
BLOCK = 32

gravity = 1.0
ratio = 0.2
source = 0.05

MESH = pl.DeviceIdType.MESH
f32 = jnp.float32
bf16 = jnp.bfloat16


def iota(shape, dim):
    return lax.broadcasted_iota(jnp.int32, shape, dim)


def weights(slip_ref, cover_ref, steps, faults, a):
    rows = -(-3 * steps // PAD) * PAD
    wide = 3 * faults
    pick_step = (iota((rows, steps), 0) // 3 == iota((rows, steps), 1)).astype(bf16)
    pick_fault = (iota((faults, wide), 1) % faults == iota((faults, wide), 0)).astype(bf16)
    slips = jnp.dot(pick_step, slip_ref[...], preferred_element_type=f32).astype(bf16)
    slips = jnp.dot(slips, pick_fault, preferred_element_type=f32)
    slot = iota((rows, wide), 0) % 3
    cover = jnp.zeros((rows, wide), f32)
    for b in range(3):
        cover = jnp.where(slot == b, cover_ref[0, 3 * a + b].astype(f32), cover)
    return jnp.where(slot == iota((rows, wide), 1) // faults, slips * cover, 0.0).astype(bf16)


def flux_terms(h, m, n):
    inv = 1.0 / h
    u = m * inv
    v = n * inv
    pressure = 0.5 * gravity * h * h
    cross = m * v
    half = 0.5 * ratio
    fx = (half * m, half * (m * u + pressure), half * cross)
    fy = (half * n, half * cross, half * (n * v + pressure))
    quarter = (0.25 * h, 0.25 * m, 0.25 * n)
    return quarter, fx, fy


def kernel(
    n_ox, n_oy,
    slip_ref, green_ref, cover_ref, wet_hbm, h_hbm, m_hbm, n_hbm,
    h_out, m_out, n_out,
    green, part, h_0, m_0, n_0, h_1, m_1, n_1, wet, fine, spread, edges, terms, terms_t,
    route_x, summed, route_y, row_out, row_in, col_out, col_in,
    green_sem, load_sem, rx_send, rx_recv, ry_send, ry_recv, row_send, row_recv, col_send, col_recv,
):
    steps, faults = slip_ref.shape
    n_rows, n_cols = wet.shape
    up_rows, up_cols = n_rows // COARSE, n_cols // COARSE
    i, j = lax.axis_index("ox"), lax.axis_index("oy")
    states = ((h_0, m_0, n_0), (h_1, m_1, n_1))
    outs = (h_out, m_out, n_out)
    near = (
        (i > 0, (i - 1, j)),
        (i < n_ox - 1, (i + 1, j)),
        (j > 0, (i, j - 1)),
        (j < n_oy - 1, (i, j + 1)),
    )

    loads = [
        pltpu.make_async_copy(src, dst, load_sem.at[q])
        for q, (src, dst) in enumerate(((h_hbm, h_0), (m_hbm, m_0), (n_hbm, n_0), (wet_hbm, wet)))
    ]
    chunks = green_sem.shape[1]
    width = green.shape[2] // chunks
    greens = {}
    for a in (2, 0, 1):
        for q in range(chunks):
            where = (pl.ds(3 * a, 3), slice(None), pl.ds(q * width, width))
            greens[a, q] = pltpu.make_async_copy(green_ref.at[where], green.at[where], green_sem.at[a, q])
            greens[a, q].start()
        if a == 2:
            for copy in loads:
                copy.start()

    barrier = pltpu.get_barrier_semaphore()
    for there, device in near:
        @pl.when(there)
        def _():
            pl.semaphore_signal(barrier, inc=1, device_id=device, device_id_type=MESH)

    zero_x = jnp.zeros(route_x.shape[2:], f32)
    zero_y = jnp.zeros(route_y.shape[2:], f32)
    for d in range(2):
        @pl.when(jnp.logical_not(near[d][0]))
        def _():
            for s in range(steps):
                route_x[s, d] = zero_x

        @pl.when(jnp.logical_not(near[2 + d][0]))
        def _():
            for s in range(steps):
                route_y[s, d] = zero_y

    coarse_of = iota((2 * up_cols, n_cols), 1) // COARSE
    spread[...] = (coarse_of == iota((2 * up_cols, n_cols), 0) % up_cols).astype(bf16)
    terms[...] = jnp.zeros(terms.shape, f32)
    row_out[...] = jnp.zeros(row_out.shape, f32)
    col_out[...] = jnp.zeros(col_out.shape, f32)
    lhs = [weights(slip_ref, cover_ref, steps, faults, a) for a in range(3)]

    pl.semaphore_wait(barrier, sum(there.astype(jnp.int32) for there, _ in near))

    def remote(src, dst, send, recv, d):
        return pltpu.make_async_remote_copy(
            src_ref=src, dst_ref=dst, send_sem=send, recv_sem=recv, device_id=near[d][1], device_id_type=MESH
        )

    def when_each(copies, what):
        for d, copy in copies:
            @pl.when(near[d ^ 1 if what == "wait_recv" else d][0])
            def _():
                getattr(copy, what)()

    def route_x_copies(s, sides=(0, 1)):
        rows = 3 * up_rows
        return [
            (d, remote(part.at[2 * d, pl.ds(s * rows, rows)], route_x.at[s, 1 - d], rx_send.at[s, d], rx_recv.at[s, 1 - d], d))
            for d in sides
        ]

    def route_y_copies(s):
        return [
            (2 + d, remote(summed.at[s, d], route_y.at[s, 1 - d], ry_send.at[s, d], ry_recv.at[s, 1 - d], 2 + d))
            for d in range(2)
        ]

    def row_copies(s):
        return [(d, remote(row_out.at[s, d], row_in.at[s, 1 - d], row_send.at[s, d], row_recv.at[s, 1 - d], d)) for d in range(2)]

    def col_copies(s):
        return [
            (2 + d, remote(col_out.at[s, d], col_in.at[s, 1 - d], col_send.at[s, d], col_recv.at[s, 1 - d], 2 + d))
            for d in range(2)
        ]

    first_block = pl.ds(0, LANES)
    last_block = pl.ds(n_cols - LANES, LANES)
    n_strips = n_rows // STRIP
    row8 = iota((STRIP, n_cols), 0)
    lane8 = iota((STRIP, LANES), 1)
    lane = iota((BLOCK, LANES), 1)

    def send_edges(s, state):
        for c in range(3):
            turned = jnp.transpose(edges[c])
            col_out[s, 0, pl.ds(c, 1)] = turned[:1]
            col_out[s, 1, pl.ds(c, 1)] = turned[LANES - 1:]
        when_each(col_copies(s), "start")

    def send_rows(s, state):
        for c in range(3):
            row_out[s, 0, pl.ds(c, 1)] = state[c][pl.ds(0, 1)]
            row_out[s, 1, pl.ds(c, 1)] = state[c][pl.ds(n_rows - 1, 1)]
        when_each(row_copies(s), "start")

    def matmul(a):
        for q in range(chunks):
            greens[a, q].wait()
            block = green[pl.ds(3 * a, 3), :, pl.ds(q * width, width)].reshape(3 * faults, width)
            out = jnp.dot(lhs[a], block, preferred_element_type=f32)
            for p in range(width // up_cols):
                row = q * (width // up_cols) + p
                part[a, pl.ds(row, out.shape[0], stride=up_rows), :] = out[:, p * up_cols:(p + 1) * up_cols]

    def pass_on(s):
        when_each(route_x_copies(s), "wait_recv")
        mine = part[1, pl.ds(s * 3 * up_rows, 3 * up_rows), :]
        total = mine + route_x[s, 0] + route_x[s, 1]
        summed[s, 0] = total[:up_rows]
        summed[s, 1] = total[2 * up_rows:]
        summed[s, 2] = total[up_rows:2 * up_rows]
        when_each(route_y_copies(s), "start")

    def lift_cells(s):
        when_each(route_y_copies(s), "wait_recv")
        lift = source * (summed[s, 2] + route_y[s, 0] + route_y[s, 1])
        high = lift.astype(bf16)
        low = (lift - high.astype(f32)).astype(bf16)
        wide = jnp.dot(jnp.concatenate([high, low], axis=1), spread[...], preferred_element_type=f32)
        for b in range(n_cols // LANES):
            for t in range(COARSE):
                fine[b, pl.ds(t, up_rows, stride=COARSE), :] = wide[:, b * LANES:(b + 1) * LANES]

    def beside(plus, minus):
        n_blocks = n_cols // LANES
        blocks = [slice(b * LANES, (b + 1) * LANES) for b in range(n_blocks)]
        after = [pltpu.roll(plus[:, block], LANES - 1, 1) for block in blocks] + [0.0]
        before = [0.0] + [pltpu.roll(minus[:, block], 1, 1) for block in blocks]
        return jnp.concatenate([
            jnp.where(lane8 == LANES - 1, after[b + 1], after[b]) + jnp.where(lane8 == 0, before[b], before[b + 1])
            for b in range(n_blocks)
        ], axis=1)

    def bulk(state, new):
        def start(base, down_before):
            quarter, fx, fy = flux_terms(*(field[pl.ds(base, STRIP)] for field in state))
            up = [pltpu.roll(quarter[c] - fx[c], STRIP - 1, 0) for c in range(3)]
            down = [pltpu.roll(quarter[c] + fx[c], 1, 0) for c in range(3)]
            sides = [beside(quarter[c] - fy[c], quarter[c] + fy[c]) for c in range(3)]
            acc = [sides[c] + jnp.where(row8 == 0, down_before[c], down[c]) for c in range(3)]
            return acc, up, down

        def store(base, acc, up, next_up):
            dry = wet[pl.ds(base, STRIP)].astype(f32)
            for c in range(3):
                value = acc[c] + jnp.where(row8 == STRIP - 1, next_up[c], up[c])
                new[c][pl.ds(base, STRIP)] = value * dry if c > 0 else value

        def group(base, carry):
            for u in range(GROUP):
                now = start(base + u * STRIP, carry[2])
                if carry[0] is not None:
                    store(base + (u - 1) * STRIP, carry[0], carry[1], now[1])
                carry = now
            return carry

        zero = jnp.zeros((STRIP, n_cols), f32)
        carry = group(0, (None, None, [zero] * 3))
        carry = lax.fori_loop(
            1, n_strips // GROUP, lambda t, carry: group(pl.multiple_of(t * GROUP * STRIP, GROUP * STRIP), carry), carry
        )
        store(n_rows - STRIP, carry[0], carry[1], [zero] * 3)

    def receive(s):
        when_each(row_copies(s), "wait_recv")
        when_each(col_copies(s), "wait_recv")
        for d in range(2):
            @pl.when(jnp.logical_not(near[d][0]))
            def _():
                row_in[s, d] = row_out[s, d]

            @pl.when(jnp.logical_not(near[2 + d][0]))
            def _():
                col_in[s, d] = col_out[s, d]

        for d in range(2):
            quarter, _, fy = flux_terms(*(col_in[s, d, pl.ds(c, 1)] for c in range(3)))
            for c in range(3):
                terms[c, pl.ds(d * (LANES - 1), 1)] = quarter[c] - fy[c] if d else quarter[c] + fy[c]
        for c in range(3):
            terms_t[c] = jnp.transpose(terms[c])

    def finish(s, new):
        for d in range(2):
            row = pl.ds(d * (n_rows - 1), 1)
            quarter, fx, _ = flux_terms(*(row_in[s, d, pl.ds(c, 1)] for c in range(3)))
            dry = wet[row].astype(f32)
            for c in range(3):
                term = quarter[c] - fx[c] if d else quarter[c] + fx[c]
                new[c][row] = new[c][row] + (term * dry if c > 0 else term)

        def body(t, carry):
            where = pl.ds(pl.multiple_of(t * BLOCK, BLOCK), BLOCK)
            dry_first = wet[where, first_block].astype(f32)
            dry_last = wet[where, last_block].astype(f32)
            for b in range(n_cols // LANES):
                block = pl.ds(b * LANES, LANES)
                new[0][where, block] = new[0][where, block] + fine[b, where]
            for c in range(3):
                term = terms_t[c, where]
                left = jnp.where(lane == 0, term, 0.0)
                right = jnp.where(lane == LANES - 1, term, 0.0)
                first = new[c][where, first_block] + (left * dry_first if c > 0 else left)
                last = new[c][where, last_block] + (right * dry_last if c > 0 else right)
                new[c][where, first_block] = first
                new[c][where, last_block] = last
                edges[c, where] = jnp.where(lane == 0, first, last)
            return carry

        lax.fori_loop(0, n_rows // BLOCK, body, 0)

    for a in (2, 0):
        matmul(a)
        for s in range(steps):
            when_each(route_x_copies(s, (a // 2,)), "start")

    for copy in loads:
        copy.wait()
    for c in range(3):
        edges[c] = jnp.where(iota((n_rows, LANES), 1) == 0, states[0][c][:, first_block], states[0][c][:, last_block])
    send_rows(0, states[0])
    send_edges(0, states[0])

    matmul(1)
    pass_on(0)
    for s in range(steps):
        state = states[s % 2]
        new = outs if s == steps - 1 else states[1 - s % 2]
        bulk(state, new)
        if s == 0:
            for later in range(1, steps):
                pass_on(later)
        lift_cells(s)
        receive(s)
        finish(s, new)
        if s < steps - 1:
            send_rows(s + 1, new)
            send_edges(s + 1, new)

    for s in range(steps):
        when_each(route_x_copies(s), "wait_send")
        when_each(route_y_copies(s), "wait_send")
        when_each(row_copies(s), "wait_send")
        when_each(col_copies(s), "wait_send")


def write_out(h, m, n, h_hbm, m_hbm, n_hbm, sems):
    copies = [
        pltpu.make_async_copy(src, dst, sems.at[q])
        for q, (src, dst) in enumerate(((h, h_hbm), (m, m_hbm), (n, n_hbm)))
    ]
    for copy in copies:
        copy.start()
    for copy in copies:
        copy.wait()


def shards(n_ox, n_oy, slip_rate, green_kernel, intersection, wet_mask, column_height, east_flow, north_flow):
    steps, faults = slip_rate.shape
    rows, cols = column_height.shape
    up_rows, up_cols = rows // COARSE, cols // COARSE
    part_rows = -(-3 * steps // PAD) * PAD * up_rows
    chunks = 4
    hbm = pl.BlockSpec(memory_space=pltpu.HBM)
    vmem = pl.BlockSpec(memory_space=pltpu.VMEM)
    dma = pltpu.SemaphoreType.DMA
    fields = [jax.ShapeDtypeStruct((rows, cols), f32)] * 3
    result = pl.pallas_call(
        functools.partial(kernel, n_ox, n_oy),
        out_shape=fields,
        in_specs=[vmem, hbm, pl.BlockSpec(memory_space=pltpu.SMEM)] + [hbm] * 4,
        out_specs=[vmem] * 3,
        scratch_shapes=[
            pltpu.VMEM((9, faults, green_kernel.shape[2]), bf16),
            pltpu.VMEM((3, part_rows, up_cols), f32),
        ] + [pltpu.VMEM((rows, cols), f32)] * 6 + [
            pltpu.VMEM((rows, cols), jnp.int32),
            pltpu.VMEM((cols // LANES, rows, LANES), f32),
            pltpu.VMEM((2 * up_cols, cols), bf16),
            pltpu.VMEM((3, rows, LANES), f32),
            pltpu.VMEM((3, LANES, rows), f32),
            pltpu.VMEM((3, rows, LANES), f32),
            pltpu.VMEM((steps, 2, 3 * up_rows, up_cols), f32),
            pltpu.VMEM((steps, 3, up_rows, up_cols), f32),
            pltpu.VMEM((steps, 2, up_rows, up_cols), f32),
            pltpu.VMEM((steps, 2, STRIP, cols), f32),
            pltpu.VMEM((steps, 2, STRIP, cols), f32),
            pltpu.VMEM((steps, 2, STRIP, rows), f32),
            pltpu.VMEM((steps, 2, STRIP, rows), f32),
            dma((3, chunks)),
            dma((4,)),
        ] + [dma((steps, 2))] * 8,
        compiler_params=pltpu.CompilerParams(
            collective_id=0, has_side_effects=True, vmem_limit_bytes=52 * 1024 * 1024
        ),
        cost_estimate=pl.CostEstimate(flops=400_000_000, bytes_accessed=16_000_000, transcendentals=0),
    )(slip_rate, green_kernel.transpose(1, 0, 2), intersection, wet_mask, column_height, east_flow, north_flow)
    return pl.pallas_call(
        write_out,
        out_shape=fields,
        in_specs=[vmem] * 3,
        out_specs=[hbm] * 3,
        scratch_shapes=[dma((3,))],
        cost_estimate=pl.CostEstimate(flops=0, bytes_accessed=6 * rows * cols * 4, transcendentals=0),
    )(*result)


def solution(mesh):
    return jax.shard_map(
        functools.partial(shards, mesh.shape["ox"], mesh.shape["oy"]),
        mesh=mesh,
        in_specs=(
            P(None, ("ox", "oy")),
            P(("ox", "oy"), None, None),
            P(("ox", "oy"), None),
            P("ox", "oy"),
            P("ox", "oy"),
            P("ox", "oy"),
            P("ox", "oy"),
        ),
        out_specs=(P("ox", "oy"), P("ox", "oy"), P("ox", "oy")),
        check_vma=False,
    )
```

```python
import functools

import jax
import jax.numpy as jnp
from jax import lax
from jax.experimental import pallas as pl
from jax.experimental.pallas import tpu as pltpu
from jax.sharding import PartitionSpec as P

COARSE = 4
STRIP = 8
LANES = 128
PAD = 16
GROUP = 8
BLOCK = 32

gravity = 1.0
ratio = 0.2
source = 0.05

MESH = pl.DeviceIdType.MESH
f32 = jnp.float32
bf16 = jnp.bfloat16


def iota(shape, dim):
    return lax.broadcasted_iota(jnp.int32, shape, dim)


def weights(slip_ref, cover_ref, steps, faults, a):
    rows = -(-3 * steps // PAD) * PAD
    wide = 3 * faults
    pick_step = (iota((rows, steps), 0) // 3 == iota((rows, steps), 1)).astype(bf16)
    pick_fault = (iota((faults, wide), 1) % faults == iota((faults, wide), 0)).astype(bf16)
    slips = jnp.dot(pick_step, slip_ref[...], preferred_element_type=f32).astype(bf16)
    slips = jnp.dot(slips, pick_fault, preferred_element_type=f32)
    slot = iota((rows, wide), 0) % 3
    cover = jnp.zeros((rows, wide), f32)
    for b in range(3):
        cover = jnp.where(slot == b, cover_ref[0, 3 * a + b].astype(f32), cover)
    return jnp.where(slot == iota((rows, wide), 1) // faults, slips * cover, 0.0).astype(bf16)


def flux_terms(h, m, n):
    half = 0.5 * ratio
    guess = pl.reciprocal(h, approx=True)
    inv = guess * (2.0 - h * guess)
    u, v = m * inv, n * inv
    east, north = half * m, half * n
    pressure = (0.5 * gravity * half * h) * h
    cross = east * v
    return (0.25 * h, 0.25 * m, 0.25 * n), (east, east * u + pressure, cross), (north, cross, north * v + pressure)


def kernel(
    n_ox, n_oy,
    slip_ref, green_ref, cover_ref, wet_hbm, h_hbm, m_hbm, n_hbm,
    h_out, m_out, n_out,
    green, part, h_0, m_0, n_0, h_1, m_1, n_1, wet, fine, spread, edges, terms, terms_t,
    route_x, summed, route_y, row_out, row_in, col_out, col_in,
    green_sem, load_sem, rx_send, rx_recv, ry_send, ry_recv, row_send, row_recv, col_send, col_recv,
):
    steps, faults = slip_ref.shape
    n_rows, n_cols = wet.shape
    up_rows, up_cols = n_rows // COARSE, n_cols // COARSE
    i, j = lax.axis_index("ox"), lax.axis_index("oy")
    states = ((h_0, m_0, n_0), (h_1, m_1, n_1))
    outs = (h_out, m_out, n_out)
    near = (
        (i > 0, (i - 1, j)),
        (i < n_ox - 1, (i + 1, j)),
        (j > 0, (i, j - 1)),
        (j < n_oy - 1, (i, j + 1)),
    )

    loads = [
        pltpu.make_async_copy(src, dst, load_sem.at[q])
        for q, (src, dst) in enumerate(((h_hbm, h_0), (m_hbm, m_0), (n_hbm, n_0), (wet_hbm, wet)))
    ]
    chunks = green_sem.shape[1]
    width = green.shape[2] // chunks
    greens = {}
    for a in (2, 0, 1):
        for q in range(chunks):
            where = (pl.ds(3 * a, 3), slice(None), pl.ds(q * width, width))
            greens[a, q] = pltpu.make_async_copy(green_ref.at[where], green.at[where], green_sem.at[a, q])
            greens[a, q].start()
        if a == 2:
            for copy in loads:
                copy.start()

    barrier = pltpu.get_barrier_semaphore()
    for there, device in near:
        @pl.when(there)
        def _():
            pl.semaphore_signal(barrier, inc=1, device_id=device, device_id_type=MESH)

    zero_x = jnp.zeros(route_x.shape[2:], f32)
    zero_y = jnp.zeros(route_y.shape[2:], f32)
    for d in range(2):
        @pl.when(jnp.logical_not(near[d][0]))
        def _():
            for s in range(steps):
                route_x[s, d] = zero_x

        @pl.when(jnp.logical_not(near[2 + d][0]))
        def _():
            for s in range(steps):
                route_y[s, d] = zero_y

    coarse_of = iota((2 * up_cols, n_cols), 1) // COARSE
    spread[...] = (coarse_of == iota((2 * up_cols, n_cols), 0) % up_cols).astype(bf16)
    terms[...] = jnp.zeros(terms.shape, f32)
    row_out[...] = jnp.zeros(row_out.shape, f32)
    col_out[...] = jnp.zeros(col_out.shape, f32)
    lhs = [weights(slip_ref, cover_ref, steps, faults, a) for a in range(3)]

    pl.semaphore_wait(barrier, sum(there.astype(jnp.int32) for there, _ in near))

    def remote(src, dst, send, recv, d):
        return pltpu.make_async_remote_copy(
            src_ref=src, dst_ref=dst, send_sem=send, recv_sem=recv, device_id=near[d][1], device_id_type=MESH
        )

    def when_each(copies, what):
        for d, copy in copies:
            @pl.when(near[d ^ 1 if what == "wait_recv" else d][0])
            def _():
                getattr(copy, what)()

    def route_x_copies(s, sides=(0, 1)):
        rows = 3 * up_rows
        return [
            (d, remote(part.at[2 * d, pl.ds(s * rows, rows)], route_x.at[s, 1 - d], rx_send.at[s, d], rx_recv.at[s, 1 - d], d))
            for d in sides
        ]

    def route_y_copies(s):
        return [
            (2 + d, remote(summed.at[s, d], route_y.at[s, 1 - d], ry_send.at[s, d], ry_recv.at[s, 1 - d], 2 + d))
            for d in range(2)
        ]

    def row_copies(s):
        return [(d, remote(row_out.at[s, d], row_in.at[s, 1 - d], row_send.at[s, d], row_recv.at[s, 1 - d], d)) for d in range(2)]

    def col_copies(s):
        return [
            (2 + d, remote(col_out.at[s, d], col_in.at[s, 1 - d], col_send.at[s, d], col_recv.at[s, 1 - d], 2 + d))
            for d in range(2)
        ]

    first_block = pl.ds(0, LANES)
    last_block = pl.ds(n_cols - LANES, LANES)
    n_strips = n_rows // STRIP
    row8 = iota((STRIP, n_cols), 0)
    lane8 = iota((STRIP, LANES), 1)
    lane = iota((BLOCK, LANES), 1)

    def send_edges(s):
        for c in range(3):
            turned = jnp.transpose(edges[c])
            col_out[s, 0, pl.ds(c, 1)] = turned[:1]
            col_out[s, 1, pl.ds(c, 1)] = turned[LANES - 1:]
        when_each(col_copies(s), "start")

    def send_rows(s, state):
        for c in range(3):
            row_out[s, 0, pl.ds(c, 1)] = state[c][pl.ds(0, 1)]
            row_out[s, 1, pl.ds(c, 1)] = state[c][pl.ds(n_rows - 1, 1)]
        when_each(row_copies(s), "start")

    def matmul(a):
        for q in range(chunks):
            greens[a, q].wait()
            block = green[pl.ds(3 * a, 3), :, pl.ds(q * width, width)].reshape(3 * faults, width)
            out = jnp.dot(lhs[a], block, preferred_element_type=f32)
            for p in range(width // up_cols):
                row = q * (width // up_cols) + p
                part[a, pl.ds(row, out.shape[0], stride=up_rows), :] = out[:, p * up_cols:(p + 1) * up_cols]

    def pass_on(s):
        when_each(route_x_copies(s), "wait_recv")
        mine = part[1, pl.ds(s * 3 * up_rows, 3 * up_rows), :]
        total = mine + route_x[s, 0] + route_x[s, 1]
        summed[s, 0] = total[:up_rows]
        summed[s, 1] = total[2 * up_rows:]
        summed[s, 2] = total[up_rows:2 * up_rows]
        when_each(route_y_copies(s), "start")

    def lift_cells(s):
        when_each(route_y_copies(s), "wait_recv")
        lift = source * (summed[s, 2] + route_y[s, 0] + route_y[s, 1])
        high = lift.astype(bf16)
        low = (lift - high.astype(f32)).astype(bf16)
        wide = jnp.dot(jnp.concatenate([high, low], axis=1), spread[...], preferred_element_type=f32)
        for b in range(n_cols // LANES):
            for t in range(COARSE):
                fine[b, pl.ds(t, up_rows, stride=COARSE), :] = wide[:, b * LANES:(b + 1) * LANES]

    def beside(plus, minus):
        n_blocks = n_cols // LANES
        blocks = [slice(b * LANES, (b + 1) * LANES) for b in range(n_blocks)]
        after = [pltpu.roll(plus[:, block], LANES - 1, 1) for block in blocks] + [0.0]
        before = [0.0] + [pltpu.roll(minus[:, block], 1, 1) for block in blocks]
        return jnp.concatenate([
            jnp.where(lane8 == LANES - 1, after[b + 1], after[b]) + jnp.where(lane8 == 0, before[b], before[b + 1])
            for b in range(n_blocks)
        ], axis=1)

    def bulk(state, new):
        def start(base, down_before):
            quarter, fx, fy = flux_terms(*(field[pl.ds(base, STRIP)] for field in state))
            up = [pltpu.roll(quarter[c] - fx[c], STRIP - 1, 0) for c in range(3)]
            down = [pltpu.roll(quarter[c] + fx[c], 1, 0) for c in range(3)]
            sides = [beside(quarter[c] - fy[c], quarter[c] + fy[c]) for c in range(3)]
            acc = [sides[c] + jnp.where(row8 == 0, down_before[c], down[c]) for c in range(3)]
            return acc, up, down

        def store(base, acc, up, next_up):
            dry = wet[pl.ds(base, STRIP)].astype(f32)
            for c in range(3):
                value = acc[c] + jnp.where(row8 == STRIP - 1, next_up[c], up[c])
                new[c][pl.ds(base, STRIP)] = value * dry if c > 0 else value

        def group(base, carry):
            for u in range(GROUP):
                now = start(base + u * STRIP, carry[2])
                if carry[0] is not None:
                    store(base + (u - 1) * STRIP, carry[0], carry[1], now[1])
                carry = now
            return carry

        zero = jnp.zeros((STRIP, n_cols), f32)
        carry = group(0, (None, None, [zero] * 3))
        carry = lax.fori_loop(
            1, n_strips // GROUP, lambda t, carry: group(pl.multiple_of(t * GROUP * STRIP, GROUP * STRIP), carry), carry
        )
        store(n_rows - STRIP, carry[0], carry[1], [zero] * 3)

    def receive(s):
        when_each(row_copies(s), "wait_recv")
        when_each(col_copies(s), "wait_recv")
        for d in range(2):
            @pl.when(jnp.logical_not(near[d][0]))
            def _():
                row_in[s, d] = row_out[s, d]

            @pl.when(jnp.logical_not(near[2 + d][0]))
            def _():
                col_in[s, d] = col_out[s, d]

        for d in range(2):
            quarter, _, fy = flux_terms(*(col_in[s, d, pl.ds(c, 1)] for c in range(3)))
            for c in range(3):
                terms[c, pl.ds(d * (LANES - 1), 1)] = quarter[c] - fy[c] if d else quarter[c] + fy[c]
        for c in range(3):
            terms_t[c] = jnp.transpose(terms[c])

    def finish(s, new):
        for d in range(2):
            row = pl.ds(d * (n_rows - 1), 1)
            quarter, fx, _ = flux_terms(*(row_in[s, d, pl.ds(c, 1)] for c in range(3)))
            dry = wet[row].astype(f32)
            for c in range(3):
                term = quarter[c] - fx[c] if d else quarter[c] + fx[c]
                new[c][row] = new[c][row] + (term * dry if c > 0 else term)

        def body(t, carry):
            where = pl.ds(pl.multiple_of(t * BLOCK, BLOCK), BLOCK)
            dry_first = wet[where, first_block].astype(f32)
            dry_last = wet[where, last_block].astype(f32)
            for b in range(n_cols // LANES):
                block = pl.ds(b * LANES, LANES)
                new[0][where, block] = new[0][where, block] + fine[b, where]
            for c in range(3):
                term = terms_t[c, where]
                left = jnp.where(lane == 0, term, 0.0)
                right = jnp.where(lane == LANES - 1, term, 0.0)
                first = new[c][where, first_block] + (left * dry_first if c > 0 else left)
                last = new[c][where, last_block] + (right * dry_last if c > 0 else right)
                new[c][where, first_block] = first
                new[c][where, last_block] = last
                if s < steps - 1:
                    edges[c, where] = jnp.where(lane == 0, first, last)
            return carry

        lax.fori_loop(0, n_rows // BLOCK, body, 0)

    for a in (2, 0):
        matmul(a)
        for s in range(steps):
            when_each(route_x_copies(s, (a // 2,)), "start")

    for copy in loads:
        copy.wait()
    for c in range(3):
        edges[c] = jnp.where(iota((n_rows, LANES), 1) == 0, states[0][c][:, first_block], states[0][c][:, last_block])
    send_rows(0, states[0])
    send_edges(0)

    matmul(1)
    pass_on(0)
    for s in range(steps):
        state = states[s % 2]
        new = outs if s == steps - 1 else states[1 - s % 2]
        bulk(state, new)
        if s == 0:
            for later in range(1, steps):
                pass_on(later)
        lift_cells(s)
        receive(s)
        finish(s, new)
        if s < steps - 1:
            send_rows(s + 1, new)
            send_edges(s + 1)

    for s in range(steps):
        when_each(route_x_copies(s), "wait_send")
        when_each(route_y_copies(s), "wait_send")
        when_each(row_copies(s), "wait_send")
        when_each(col_copies(s), "wait_send")


def write_out(h, m, n, h_hbm, m_hbm, n_hbm, sems):
    copies = [
        pltpu.make_async_copy(src, dst, sems.at[q])
        for q, (src, dst) in enumerate(((h, h_hbm), (m, m_hbm), (n, n_hbm)))
    ]
    for copy in copies:
        copy.start()
    for copy in copies:
        copy.wait()


def shards(n_ox, n_oy, slip_rate, green_kernel, intersection, wet_mask, column_height, east_flow, north_flow):
    steps, faults = slip_rate.shape
    rows, cols = column_height.shape
    up_rows, up_cols = rows // COARSE, cols // COARSE
    part_rows = -(-3 * steps // PAD) * PAD * up_rows
    chunks = 4
    hbm = pl.BlockSpec(memory_space=pltpu.HBM)
    vmem = pl.BlockSpec(memory_space=pltpu.VMEM)
    dma = pltpu.SemaphoreType.DMA
    fields = [jax.ShapeDtypeStruct((rows, cols), f32)] * 3
    result = pl.pallas_call(
        functools.partial(kernel, n_ox, n_oy),
        out_shape=fields,
        in_specs=[vmem, hbm, pl.BlockSpec(memory_space=pltpu.SMEM)] + [hbm] * 4,
        out_specs=[vmem] * 3,
        scratch_shapes=[
            pltpu.VMEM((9, faults, green_kernel.shape[2]), bf16),
            pltpu.VMEM((3, part_rows, up_cols), f32),
        ] + [pltpu.VMEM((rows, cols), f32)] * 6 + [
            pltpu.VMEM((rows, cols), jnp.int32),
            pltpu.VMEM((cols // LANES, rows, LANES), f32),
            pltpu.VMEM((2 * up_cols, cols), bf16),
            pltpu.VMEM((3, rows, LANES), f32),
            pltpu.VMEM((3, LANES, rows), f32),
            pltpu.VMEM((3, rows, LANES), f32),
            pltpu.VMEM((steps, 2, 3 * up_rows, up_cols), f32),
            pltpu.VMEM((steps, 3, up_rows, up_cols), f32),
            pltpu.VMEM((steps, 2, up_rows, up_cols), f32),
            pltpu.VMEM((steps, 2, STRIP, cols), f32),
            pltpu.VMEM((steps, 2, STRIP, cols), f32),
            pltpu.VMEM((steps, 2, STRIP, rows), f32),
            pltpu.VMEM((steps, 2, STRIP, rows), f32),
            dma((3, chunks)),
            dma((4,)),
        ] + [dma((steps, 2))] * 8,
        compiler_params=pltpu.CompilerParams(
            collective_id=0, has_side_effects=True, vmem_limit_bytes=52 * 1024 * 1024
        ),
        cost_estimate=pl.CostEstimate(flops=400_000_000, bytes_accessed=16_000_000, transcendentals=0),
    )(slip_rate, green_kernel.transpose(1, 0, 2), intersection, wet_mask, column_height, east_flow, north_flow)
    return pl.pallas_call(
        write_out,
        out_shape=fields,
        in_specs=[vmem] * 3,
        out_specs=[hbm] * 3,
        scratch_shapes=[dma((3,))],
        compiler_params=pltpu.CompilerParams(vmem_limit_bytes=4 * 1024 * 1024),
        cost_estimate=pl.CostEstimate(flops=0, bytes_accessed=6 * rows * cols * 4, transcendentals=0),
    )(*result)


def solution(mesh):
    return jax.shard_map(
        functools.partial(shards, mesh.shape["ox"], mesh.shape["oy"]),
        mesh=mesh,
        in_specs=(
            P(None, ("ox", "oy")),
            P(("ox", "oy"), None, None),
            P(("ox", "oy"), None),
            P("ox", "oy"),
            P("ox", "oy"),
            P("ox", "oy"),
            P("ox", "oy"),
        ),
        out_specs=(P("ox", "oy"), P("ox", "oy"), P("ox", "oy")),
        check_vma=False,
    )
```

```python
import functools

import jax
import jax.numpy as jnp
from jax import lax
from jax.experimental import pallas as pl
from jax.experimental.pallas import tpu as pltpu
from jax.sharding import PartitionSpec as P

COARSE = 4
STRIP = 8
LANES = 128
PAD = 16
GROUP = 8
BLOCK = 32

gravity = 1.0
ratio = 0.2
source = 0.05

MESH = pl.DeviceIdType.MESH
f32 = jnp.float32
bf16 = jnp.bfloat16


def iota(shape, dim):
    return lax.broadcasted_iota(jnp.int32, shape, dim)


def weights(slip_ref, cover_ref, steps, faults, a):
    rows = -(-3 * steps // PAD) * PAD
    wide = 3 * faults
    pick_step = (iota((rows, steps), 0) // 3 == iota((rows, steps), 1)).astype(bf16)
    pick_fault = (iota((faults, wide), 1) % faults == iota((faults, wide), 0)).astype(bf16)
    slips = jnp.dot(pick_step, slip_ref[...], preferred_element_type=f32).astype(bf16)
    slips = jnp.dot(slips, pick_fault, preferred_element_type=f32)
    slot = iota((rows, wide), 0) % 3
    cover = jnp.zeros((rows, wide), f32)
    for b in range(3):
        cover = jnp.where(slot == b, cover_ref[0, 3 * a + b].astype(f32), cover)
    return jnp.where(slot == iota((rows, wide), 1) // faults, slips * cover, 0.0).astype(bf16)


def flux_terms(h, m, n):
    half = 0.5 * ratio
    guess = pl.reciprocal(h, approx=True)
    inv = guess * (2.0 - h * guess)
    u, v = m * inv, n * inv
    east, north = half * m, half * n
    pressure = (0.5 * gravity * half * h) * h
    cross = east * v
    return (0.25 * h, 0.25 * m, 0.25 * n), (east, east * u + pressure, cross), (north, cross, north * v + pressure)


def kernel(
    n_ox, n_oy,
    slip_ref, green_ref, cover_ref, wet_hbm, h_hbm, m_hbm, n_hbm,
    h_out, m_out, n_out,
    green, part, h_0, m_0, n_0, h_1, m_1, n_1, wet, fine, spread, terms, terms_t,
    route_x, summed, route_y, row_out, row_in, col_out, col_in,
    green_sem, load_sem, rx_send, rx_recv, ry_send, ry_recv, row_send, row_recv, col_send, col_recv,
):
    steps, faults = slip_ref.shape
    n_rows, n_cols = wet.shape
    up_rows, up_cols = n_rows // COARSE, n_cols // COARSE
    i, j = lax.axis_index("ox"), lax.axis_index("oy")
    states = ((h_0, m_0, n_0), (h_1, m_1, n_1))
    outs = (h_out, m_out, n_out)
    near = (
        (i > 0, (i - 1, j)),
        (i < n_ox - 1, (i + 1, j)),
        (j > 0, (i, j - 1)),
        (j < n_oy - 1, (i, j + 1)),
    )

    loads = [
        pltpu.make_async_copy(src, dst, load_sem.at[q])
        for q, (src, dst) in enumerate(((h_hbm, h_0), (m_hbm, m_0), (n_hbm, n_0), (wet_hbm, wet)))
    ]
    chunks = green_sem.shape[1]
    width = green.shape[2] // chunks
    greens = {}
    for a in (2, 0, 1):
        for q in range(chunks):
            where = (pl.ds(3 * a, 3), slice(None), pl.ds(q * width, width))
            greens[a, q] = pltpu.make_async_copy(green_ref.at[where], green.at[where], green_sem.at[a, q])
            greens[a, q].start()
        if a == 2:
            for copy in loads:
                copy.start()

    barrier = pltpu.get_barrier_semaphore()
    for there, device in near:
        @pl.when(there)
        def _():
            pl.semaphore_signal(barrier, inc=1, device_id=device, device_id_type=MESH)

    zero_x = jnp.zeros(route_x.shape[2:], f32)
    zero_y = jnp.zeros(route_y.shape[2:], f32)
    for d in range(2):
        @pl.when(jnp.logical_not(near[d][0]))
        def _():
            for s in range(steps):
                route_x[s, d] = zero_x

        @pl.when(jnp.logical_not(near[2 + d][0]))
        def _():
            for s in range(steps):
                route_y[s, d] = zero_y

    coarse_of = iota((2 * up_cols, n_cols), 1) // COARSE
    spread[...] = (coarse_of == iota((2 * up_cols, n_cols), 0) % up_cols).astype(bf16)
    terms[...] = jnp.zeros(terms.shape, f32)
    row_out[...] = jnp.zeros(row_out.shape, f32)
    col_out[...] = jnp.zeros(col_out.shape, f32)
    lhs = [weights(slip_ref, cover_ref, steps, faults, a) for a in range(3)]

    pl.semaphore_wait(barrier, sum(there.astype(jnp.int32) for there, _ in near))

    def remote(src, dst, send, recv, d):
        return pltpu.make_async_remote_copy(
            src_ref=src, dst_ref=dst, send_sem=send, recv_sem=recv, device_id=near[d][1], device_id_type=MESH
        )

    def when_each(copies, what):
        for d, copy in copies:
            @pl.when(near[d ^ 1 if what == "wait_recv" else d][0])
            def _():
                getattr(copy, what)()

    def route_x_copies(s, sides=(0, 1)):
        rows = 3 * up_rows
        return [
            (d, remote(part.at[2 * d, pl.ds(s * rows, rows)], route_x.at[s, 1 - d], rx_send.at[s, d], rx_recv.at[s, 1 - d], d))
            for d in sides
        ]

    def route_y_copies(s):
        return [
            (2 + d, remote(summed.at[s, d], route_y.at[s, 1 - d], ry_send.at[s, d], ry_recv.at[s, 1 - d], 2 + d))
            for d in range(2)
        ]

    def row_copies(s):
        return [(d, remote(row_out.at[s, d], row_in.at[s, 1 - d], row_send.at[s, d], row_recv.at[s, 1 - d], d)) for d in range(2)]

    def col_copies(s):
        return [
            (2 + d, remote(col_out.at[s, d], col_in.at[s, 1 - d], col_send.at[s, d], col_recv.at[s, 1 - d], 2 + d))
            for d in range(2)
        ]

    first_block = pl.ds(0, LANES)
    last_block = pl.ds(n_cols - LANES, LANES)
    n_strips = n_rows // STRIP
    row8 = iota((STRIP, n_cols), 0)
    lane8 = iota((STRIP, LANES), 1)
    lane = iota((BLOCK, LANES), 1)

    def send(s, state, packed):
        for c in range(3):
            row_out[s, 0, pl.ds(c, 1)] = state[c][pl.ds(0, 1)]
            row_out[s, 1, pl.ds(c, 1)] = state[c][pl.ds(n_rows - 1, 1)]
            for t in range(n_rows // LANES):
                where = pl.ds(t * LANES, LANES)
                turned = jnp.transpose(packed[c][t])
                col_out[s, 0, pl.ds(c, 1), where] = turned[:1]
                col_out[s, 1, pl.ds(c, 1), where] = turned[LANES - 1:]
        when_each(row_copies(s), "start")
        when_each(col_copies(s), "start")
        for d in range(2):
            @pl.when(jnp.logical_not(near[d][0]))
            def _():
                row_in[s, d] = row_out[s, d]

            @pl.when(jnp.logical_not(near[2 + d][0]))
            def _():
                col_in[s, d] = col_out[s, d]

    def matmul(a):
        for q in range(chunks):
            greens[a, q].wait()
            block = green[pl.ds(3 * a, 3), :, pl.ds(q * width, width)].reshape(3 * faults, width)
            out = jnp.dot(lhs[a], block, preferred_element_type=f32)
            for p in range(width // up_cols):
                row = q * (width // up_cols) + p
                part[a, pl.ds(row, out.shape[0], stride=up_rows), :] = out[:, p * up_cols:(p + 1) * up_cols]

    def pass_on(s):
        when_each(route_x_copies(s), "wait_recv")
        mine = part[1, pl.ds(s * 3 * up_rows, 3 * up_rows), :]
        total = mine + route_x[s, 0] + route_x[s, 1]
        summed[s, 0] = total[:up_rows]
        summed[s, 1] = total[2 * up_rows:]
        summed[s, 2] = total[up_rows:2 * up_rows]
        when_each(route_y_copies(s), "start")

    def lift_cells(s):
        lift = source * (summed[s, 2] + route_y[s, 0] + route_y[s, 1])
        high = lift.astype(bf16)
        low = (lift - high.astype(f32)).astype(bf16)
        wide = jnp.dot(jnp.concatenate([high, low], axis=1), spread[...], preferred_element_type=f32)
        for b in range(n_cols // LANES):
            for t in range(COARSE):
                fine[b, pl.ds(t, up_rows, stride=COARSE), :] = wide[:, b * LANES:(b + 1) * LANES]

    def beside(plus, minus):
        n_blocks = n_cols // LANES
        blocks = [slice(b * LANES, (b + 1) * LANES) for b in range(n_blocks)]
        after = [pltpu.roll(plus[:, block], LANES - 1, 1) for block in blocks] + [0.0]
        before = [0.0] + [pltpu.roll(minus[:, block], 1, 1) for block in blocks]
        return jnp.concatenate([
            jnp.where(lane8 == LANES - 1, after[b + 1], after[b]) + jnp.where(lane8 == 0, before[b], before[b + 1])
            for b in range(n_blocks)
        ], axis=1)

    def bulk(state, new, wait, beside_last):
        def start(base, down_before):
            quarter, fx, fy = flux_terms(*(field[pl.ds(base, STRIP)] for field in state))
            up = [pltpu.roll(quarter[c] - fx[c], STRIP - 1, 0) for c in range(3)]
            down = [pltpu.roll(quarter[c] + fx[c], 1, 0) for c in range(3)]
            sides = [beside(quarter[c] - fy[c], quarter[c] + fy[c]) for c in range(3)]
            acc = [sides[c] + jnp.where(row8 == 0, down_before[c], down[c]) for c in range(3)]
            return acc, up, down

        def store(base, acc, up, next_up):
            dry = wet[pl.ds(base, STRIP)].astype(f32)
            for c in range(3):
                value = acc[c] + jnp.where(row8 == STRIP - 1, next_up[c], up[c])
                new[c][pl.ds(base, STRIP)] = value * dry if c > 0 else value

        def group(base, carry):
            for u in range(GROUP):
                now = start(base + u * STRIP, carry[2])
                if carry[0] is not None:
                    store(base + (u - 1) * STRIP, carry[0], carry[1], now[1])
                carry = now
            return carry

        zero = jnp.zeros((STRIP, n_cols), f32)
        carry = group(0, (None, None, [zero] * 3))
        carry = lax.fori_loop(
            1, n_strips // GROUP - 1, lambda t, carry: group(pl.multiple_of(t * GROUP * STRIP, GROUP * STRIP), carry), carry
        )
        wait()
        beside_last()
        carry = group(n_rows - GROUP * STRIP, carry)
        store(n_rows - STRIP, carry[0], carry[1], [zero] * 3)

    def wait_edges(s):
        when_each(row_copies(s), "wait_recv")
        when_each(col_copies(s), "wait_recv")

    def receive(s):
        for d in range(2):
            quarter, _, fy = flux_terms(*(col_in[s, d, pl.ds(c, 1)] for c in range(3)))
            for c in range(3):
                terms[c, pl.ds(d * (LANES - 1), 1)] = quarter[c] - fy[c] if d else quarter[c] + fy[c]
        for c in range(3):
            terms_t[c] = jnp.transpose(terms[c])

    def finish(s, new):
        for d in range(2):
            row = pl.ds(d * (n_rows - 1), 1)
            quarter, fx, _ = flux_terms(*(row_in[s, d, pl.ds(c, 1)] for c in range(3)))
            dry = wet[row].astype(f32)
            for c in range(3):
                term = quarter[c] - fx[c] if d else quarter[c] + fx[c]
                new[c][row] = new[c][row] + (term * dry if c > 0 else term)

        packed = [[], [], []]
        for t in range(n_rows // LANES):
            pieces = [[], [], []]
            for u in range(LANES // BLOCK):
                where = pl.ds(t * LANES + u * BLOCK, BLOCK)
                dry_first = wet[where, first_block].astype(f32)
                dry_last = wet[where, last_block].astype(f32)
                for b in range(n_cols // LANES):
                    block = pl.ds(b * LANES, LANES)
                    new[0][where, block] = new[0][where, block] + fine[b, where]
                for c in range(3):
                    term = terms_t[c, where]
                    left = jnp.where(lane == 0, term, 0.0)
                    right = jnp.where(lane == LANES - 1, term, 0.0)
                    first = new[c][where, first_block] + (left * dry_first if c > 0 else left)
                    last = new[c][where, last_block] + (right * dry_last if c > 0 else right)
                    new[c][where, first_block] = first
                    new[c][where, last_block] = last
                    pieces[c].append(jnp.where(lane == 0, first, last))
            for c in range(3):
                packed[c].append(jnp.concatenate(pieces[c], axis=0))
        return packed

    for a in (2, 0):
        matmul(a)
        for s in range(steps):
            when_each(route_x_copies(s, (a // 2,)), "start")

    for copy in loads:
        copy.wait()
    lane_tile = iota((LANES, LANES), 1)
    send(0, states[0], [
        [
            jnp.where(lane_tile == 0, field[pl.ds(t * LANES, LANES), first_block], field[pl.ds(t * LANES, LANES), last_block])
            for t in range(n_rows // LANES)
        ]
        for field in states[0]
    ])

    matmul(1)
    pass_on(0)
    for s in range(steps):
        state = states[s % 2]
        new = outs if s == steps - 1 else states[1 - s % 2]

        def wait():
            wait_edges(s)
            if s > 0:
                when_each(route_y_copies(s), "wait_recv")

        def beside_last():
            receive(s)
            if s > 0:
                lift_cells(s)

        bulk(state, new, wait, beside_last)
        if s == 0:
            for later in range(1, steps):
                pass_on(later)
            when_each(route_y_copies(0), "wait_recv")
            lift_cells(0)
        packed = finish(s, new)
        if s < steps - 1:
            send(s + 1, new, packed)

    for s in range(steps):
        when_each(route_x_copies(s), "wait_send")
        when_each(route_y_copies(s), "wait_send")
        when_each(row_copies(s), "wait_send")
        when_each(col_copies(s), "wait_send")


def write_out(h, m, n, h_hbm, m_hbm, n_hbm, sems):
    copies = [
        pltpu.make_async_copy(src, dst, sems.at[q])
        for q, (src, dst) in enumerate(((h, h_hbm), (m, m_hbm), (n, n_hbm)))
    ]
    for copy in copies:
        copy.start()
    for copy in copies:
        copy.wait()


def shards(n_ox, n_oy, slip_rate, green_kernel, intersection, wet_mask, column_height, east_flow, north_flow):
    steps, faults = slip_rate.shape
    rows, cols = column_height.shape
    up_rows, up_cols = rows // COARSE, cols // COARSE
    part_rows = -(-3 * steps // PAD) * PAD * up_rows
    chunks = 4
    hbm = pl.BlockSpec(memory_space=pltpu.HBM)
    vmem = pl.BlockSpec(memory_space=pltpu.VMEM)
    dma = pltpu.SemaphoreType.DMA
    fields = [jax.ShapeDtypeStruct((rows, cols), f32)] * 3
    result = pl.pallas_call(
        functools.partial(kernel, n_ox, n_oy),
        out_shape=fields,
        in_specs=[vmem, hbm, pl.BlockSpec(memory_space=pltpu.SMEM)] + [hbm] * 4,
        out_specs=[vmem] * 3,
        scratch_shapes=[
            pltpu.VMEM((9, faults, green_kernel.shape[2]), bf16),
            pltpu.VMEM((3, part_rows, up_cols), f32),
        ] + [pltpu.VMEM((rows, cols), f32)] * 6 + [
            pltpu.VMEM((rows, cols), jnp.int32),
            pltpu.VMEM((cols // LANES, rows, LANES), f32),
            pltpu.VMEM((2 * up_cols, cols), bf16),
            pltpu.VMEM((3, LANES, rows), f32),
            pltpu.VMEM((3, rows, LANES), f32),
            pltpu.VMEM((steps, 2, 3 * up_rows, up_cols), f32),
            pltpu.VMEM((steps, 3, up_rows, up_cols), f32),
            pltpu.VMEM((steps, 2, up_rows, up_cols), f32),
            pltpu.VMEM((steps, 2, STRIP, cols), f32),
            pltpu.VMEM((steps, 2, STRIP, cols), f32),
            pltpu.VMEM((steps, 2, STRIP, rows), f32),
            pltpu.VMEM((steps, 2, STRIP, rows), f32),
            dma((3, chunks)),
            dma((4,)),
        ] + [dma((steps, 2))] * 8,
        compiler_params=pltpu.CompilerParams(
            collective_id=0, has_side_effects=True, vmem_limit_bytes=52 * 1024 * 1024
        ),
        cost_estimate=pl.CostEstimate(flops=400_000_000, bytes_accessed=16_000_000, transcendentals=0),
    )(slip_rate, green_kernel.transpose(1, 0, 2), intersection, wet_mask, column_height, east_flow, north_flow)
    return pl.pallas_call(
        write_out,
        out_shape=fields,
        in_specs=[vmem] * 3,
        out_specs=[hbm] * 3,
        scratch_shapes=[dma((3,))],
        compiler_params=pltpu.CompilerParams(vmem_limit_bytes=4 * 1024 * 1024),
        cost_estimate=pl.CostEstimate(flops=0, bytes_accessed=6 * rows * cols * 4, transcendentals=0),
    )(*result)


def solution(mesh):
    return jax.shard_map(
        functools.partial(shards, mesh.shape["ox"], mesh.shape["oy"]),
        mesh=mesh,
        in_specs=(
            P(None, ("ox", "oy")),
            P(("ox", "oy"), None, None),
            P(("ox", "oy"), None),
            P("ox", "oy"),
            P("ox", "oy"),
            P("ox", "oy"),
            P("ox", "oy"),
        ),
        out_specs=(P("ox", "oy"), P("ox", "oy"), P("ox", "oy")),
        check_vma=False,
    )
```

```python
import functools

import jax
import jax.numpy as jnp
from jax import lax
from jax.experimental import pallas as pl
from jax.experimental.pallas import tpu as pltpu
from jax.sharding import PartitionSpec as P

COARSE = 4
STRIP = 8
LANES = 128
PAD = 16
GROUP = 8
BLOCK = 32

gravity = 1.0
ratio = 0.2
source = 0.05

MESH = pl.DeviceIdType.MESH
f32 = jnp.float32
bf16 = jnp.bfloat16


def iota(shape, dim):
    return lax.broadcasted_iota(jnp.int32, shape, dim)


def weights(slip_ref, cover_ref, steps, faults, a):
    rows = -(-3 * steps // PAD) * PAD
    wide = 3 * faults
    pick_step = (iota((rows, steps), 0) // 3 == iota((rows, steps), 1)).astype(bf16)
    pick_fault = (iota((faults, wide), 1) % faults == iota((faults, wide), 0)).astype(bf16)
    slips = jnp.dot(pick_step, slip_ref[...], preferred_element_type=f32).astype(bf16)
    slips = jnp.dot(slips, pick_fault, preferred_element_type=f32)
    slot = iota((rows, wide), 0) % 3
    cover = jnp.zeros((rows, wide), f32)
    for b in range(3):
        cover = jnp.where(slot == b, cover_ref[0, 3 * a + b].astype(f32), cover)
    return jnp.where(slot == iota((rows, wide), 1) // faults, slips * cover, 0.0).astype(bf16)


def flux_terms(h, m, n):
    half = 0.5 * ratio
    guess = pl.reciprocal(h, approx=True)
    inv = guess * (2.0 - h * guess)
    u, v = m * inv, n * inv
    east, north = half * m, half * n
    pressure = (0.5 * gravity * half * h) * h
    cross = east * v
    return (0.25 * h, 0.25 * m, 0.25 * n), (east, east * u + pressure, cross), (north, cross, north * v + pressure)


def kernel(
    n_ox, n_oy,
    slip_ref, green_ref, cover_ref, wet_hbm, h_hbm, m_hbm, n_hbm,
    h_out, m_out, n_out,
    green, part, h_1, m_1, n_1, wet, fine, spread, edges, terms, terms_t, lhs,
    route_x, summed, route_y, row_out, row_in, col_out, col_in,
    green_sem, load_sem, rx_send, rx_recv, ry_send, ry_recv, row_send, row_recv, col_send, col_recv,
):
    steps, faults = slip_ref.shape
    n_rows, n_cols = wet.shape
    up_rows, up_cols = n_rows // COARSE, n_cols // COARSE
    i, j = lax.axis_index("ox"), lax.axis_index("oy")
    states = ((h_out, m_out, n_out), (h_1, m_1, n_1))
    near = (
        (i > 0, (i - 1, j)),
        (i < n_ox - 1, (i + 1, j)),
        (j > 0, (i, j - 1)),
        (j < n_oy - 1, (i, j + 1)),
    )

    loads = [
        pltpu.make_async_copy(src, dst, load_sem.at[q])
        for q, (src, dst) in enumerate(((h_hbm, h_out), (m_hbm, m_out), (n_hbm, n_out), (wet_hbm, wet)))
    ]
    chunks = green_sem.shape[1]
    width = green.shape[2] // chunks

    def green_copy(a, q):
        where = (pl.ds(3 * a, 3), slice(None), pl.ds(pl.multiple_of(q * width, width), width))
        return pltpu.make_async_copy(green_ref.at[where], green.at[where], green_sem.at[a, q])

    def load_slots(o, carry):
        a = lax.rem(o + 2, 3)
        for q in range(chunks):
            green_copy(a, q).start()
        return carry

    load_slots(0, 0)
    for copy in loads:
        copy.start()
    lax.fori_loop(1, 3, load_slots, 0)

    barrier = pltpu.get_barrier_semaphore()
    for there, device in near:
        @pl.when(there)
        def _():
            pl.semaphore_signal(barrier, inc=1, device_id=device, device_id_type=MESH)

    zero_x = jnp.zeros(route_x.shape[2:], f32)
    zero_y = jnp.zeros(route_y.shape[2:], f32)
    for d in range(2):
        @pl.when(jnp.logical_not(near[d][0]))
        def _():
            for s in range(steps):
                route_x[s, d] = zero_x

        @pl.when(jnp.logical_not(near[2 + d][0]))
        def _():
            for s in range(steps):
                route_y[s, d] = zero_y

    coarse_of = iota((2 * up_cols, n_cols), 1) // COARSE
    spread[...] = (coarse_of == iota((2 * up_cols, n_cols), 0) % up_cols).astype(bf16)
    terms[...] = jnp.zeros(terms.shape, f32)
    row_out[...] = jnp.zeros(row_out.shape, f32)
    col_out[...] = jnp.zeros(col_out.shape, f32)
    for a in range(3):
        lhs[a] = weights(slip_ref, cover_ref, steps, faults, a)

    pl.semaphore_wait(barrier, sum(there.astype(jnp.int32) for there, _ in near))

    def remote(src, dst, send, recv, d):
        return pltpu.make_async_remote_copy(
            src_ref=src, dst_ref=dst, send_sem=send, recv_sem=recv, device_id=near[d][1], device_id_type=MESH
        )

    def when_each(copies, what):
        sides = {}
        for d, copy in copies:
            sides.setdefault(d ^ 1 if what == "wait_recv" else d, []).append(copy)
        for d, some in sides.items():
            @pl.when(near[d][0])
            def _():
                for copy in some:
                    getattr(copy, what)()

    def route_x_copies(s, sides=(0, 1)):
        rows = 3 * up_rows
        return [
            (d, remote(part.at[2 * d, pl.ds(s * rows, rows)], route_x.at[s, 1 - d], rx_send.at[s, d], rx_recv.at[s, 1 - d], d))
            for d in sides
        ]

    def route_y_copies(s):
        return [
            (2 + d, remote(summed.at[s, d], route_y.at[s, 1 - d], ry_send.at[s, d], ry_recv.at[s, 1 - d], 2 + d))
            for d in range(2)
        ]

    def row_copies(s):
        return [(d, remote(row_out.at[s, d], row_in.at[s, 1 - d], row_send.at[s, d], row_recv.at[s, 1 - d], d)) for d in range(2)]

    def col_copies(s):
        return [
            (2 + d, remote(col_out.at[s, d], col_in.at[s, 1 - d], col_send.at[s, d], col_recv.at[s, 1 - d], 2 + d))
            for d in range(2)
        ]

    first_block = pl.ds(0, LANES)
    last_block = pl.ds(n_cols - LANES, LANES)
    n_strips = n_rows // STRIP
    row8 = iota((STRIP, n_cols), 0)
    lane8 = iota((STRIP, LANES), 1)
    lane = iota((BLOCK, LANES), 1)

    def send(s, state):
        for c in range(3):
            row_out[s, 0, pl.ds(c, 1)] = state[c][pl.ds(0, 1)]
            row_out[s, 1, pl.ds(c, 1)] = state[c][pl.ds(n_rows - 1, 1)]
            turned = jnp.transpose(edges[c])
            col_out[s, 0, pl.ds(c, 1)] = turned[:1]
            col_out[s, 1, pl.ds(c, 1)] = turned[LANES - 1:]
        when_each(row_copies(s) + col_copies(s), "start")

    def matmul(a):
        def body(q, carry):
            green_copy(a, q).wait()
            where = pl.ds(pl.multiple_of(q * width, width), width)
            block = green[pl.ds(3 * a, 3), :, where].reshape(3 * faults, width)
            out = jnp.dot(lhs[a], block, preferred_element_type=f32)
            for p in range(width // up_cols):
                row = q * (width // up_cols) + p
                part[a, pl.ds(row, out.shape[0], stride=up_rows), :] = out[:, p * up_cols:(p + 1) * up_cols]
            return carry

        lax.fori_loop(0, chunks, body, 0)

    def pass_on(s):
        when_each(route_x_copies(s), "wait_recv")
        mine = part[1, pl.ds(s * 3 * up_rows, 3 * up_rows), :]
        total = mine + route_x[s, 0] + route_x[s, 1]
        summed[s, 0] = total[:up_rows]
        summed[s, 1] = total[2 * up_rows:]
        summed[s, 2] = total[up_rows:2 * up_rows]
        when_each(route_y_copies(s), "start")

    def lift_cells(s):
        when_each(route_y_copies(s), "wait_recv")
        lift = source * (summed[s, 2] + route_y[s, 0] + route_y[s, 1])
        high = lift.astype(bf16)
        low = (lift - high.astype(f32)).astype(bf16)
        wide = jnp.dot(jnp.concatenate([high, low], axis=1), spread[...], preferred_element_type=f32)
        for b in range(n_cols // LANES):
            for t in range(COARSE):
                fine[b, pl.ds(t, up_rows, stride=COARSE), :] = wide[:, b * LANES:(b + 1) * LANES]

    def beside(plus, minus):
        n_blocks = n_cols // LANES
        blocks = [slice(b * LANES, (b + 1) * LANES) for b in range(n_blocks)]
        after = [pltpu.roll(plus[:, block], LANES - 1, 1) for block in blocks] + [0.0]
        before = [0.0] + [pltpu.roll(minus[:, block], 1, 1) for block in blocks]
        return jnp.concatenate([
            jnp.where(lane8 == LANES - 1, after[b + 1], after[b]) + jnp.where(lane8 == 0, before[b], before[b + 1])
            for b in range(n_blocks)
        ], axis=1)

    def bulk(state, new):
        def rows(base):
            quarter, fx, fy = flux_terms(*(field[pl.ds(base, STRIP)] for field in state))
            return quarter, fx, fy, [pltpu.roll(quarter[c] - fx[c], STRIP - 1, 0) for c in range(3)]

        def group(t, down_before):
            first = pl.multiple_of(t * GROUP * STRIP, GROUP * STRIP)
            now = rows(first)
            for u in range(GROUP):
                base = first + u * STRIP
                if u < GROUP - 1:
                    later = rows(base + STRIP)
                    next_up = later[3]
                else:
                    inside = base + STRIP < n_rows
                    later = rows(pl.multiple_of(jnp.where(inside, base + STRIP, base), STRIP))
                    next_up = [jnp.where(inside, value, 0.0) for value in later[3]]
                quarter, fx, fy, up = now
                dry = wet[pl.ds(base, STRIP)].astype(f32)
                down = [pltpu.roll(quarter[c] + fx[c], 1, 0) for c in range(3)]
                for c in range(3):
                    value = beside(quarter[c] - fy[c], quarter[c] + fy[c])
                    value += jnp.where(row8 == 0, down_before[c], down[c])
                    value += jnp.where(row8 == STRIP - 1, next_up[c], up[c])
                    new[c][pl.ds(base, STRIP)] = value * dry if c > 0 else value
                now, down_before = later, down
            return down_before

        lax.fori_loop(0, n_strips // GROUP, group, [jnp.zeros((STRIP, n_cols), f32)] * 3)

    def receive(s):
        when_each(row_copies(s) + col_copies(s), "wait_recv")
        for d in range(2):
            @pl.when(jnp.logical_not(near[d][0]))
            def _():
                row_in[s, d] = row_out[s, d]

            @pl.when(jnp.logical_not(near[2 + d][0]))
            def _():
                col_in[s, d] = col_out[s, d]

        for d in range(2):
            quarter, _, fy = flux_terms(*(col_in[s, d, pl.ds(c, 1)] for c in range(3)))
            for c in range(3):
                terms[c, pl.ds(d * (LANES - 1), 1)] = quarter[c] - fy[c] if d else quarter[c] + fy[c]
        for c in range(3):
            terms_t[c] = jnp.transpose(terms[c])

    def finish(s, new):
        for d in range(2):
            row = pl.ds(d * (n_rows - 1), 1)
            quarter, fx, _ = flux_terms(*(row_in[s, d, pl.ds(c, 1)] for c in range(3)))
            dry = wet[row].astype(f32)
            for c in range(3):
                term = quarter[c] - fx[c] if d else quarter[c] + fx[c]
                new[c][row] = new[c][row] + (term * dry if c > 0 else term)

        def body(t, carry):
            where = pl.ds(pl.multiple_of(t * BLOCK, BLOCK), BLOCK)
            dry_first = wet[where, first_block].astype(f32)
            dry_last = wet[where, last_block].astype(f32)
            for b in range(n_cols // LANES):
                block = pl.ds(b * LANES, LANES)
                new[0][where, block] = new[0][where, block] + fine[b, where]
            for c in range(3):
                term = terms_t[c, where]
                left = jnp.where(lane == 0, term, 0.0)
                right = jnp.where(lane == LANES - 1, term, 0.0)
                first = new[c][where, first_block] + (left * dry_first if c > 0 else left)
                last = new[c][where, last_block] + (right * dry_last if c > 0 else right)
                new[c][where, first_block] = first
                new[c][where, last_block] = last
                edges[c, where] = jnp.where(lane == 0, first, last)
            return carry

        lax.fori_loop(0, n_rows // BLOCK, body, 0)

    def slots(o, carry):
        a = lax.rem(o + 2, 3)
        matmul(a)
        for d in range(2):
            @pl.when(jnp.logical_and(a == 2 * d, near[d][0]))
            def _():
                for s in range(steps):
                    route_x_copies(s, (d,))[0][1].start()
        return carry

    lax.fori_loop(0, 2, slots, 0)
    for copy in loads:
        copy.wait()
    for c in range(3):
        edges[c] = jnp.where(iota((n_rows, LANES), 1) == 0, states[0][c][:, first_block], states[0][c][:, last_block])
    send(0, states[0])
    lax.fori_loop(2, 3, slots, 0)
    pass_on(0)

    def pair(t, carry):
        for half in range(2):
            s = 2 * t + half
            new = states[1 - half]
            bulk(states[half], new)
            if half == 0:
                @pl.when(t == 0)
                def _():
                    def later(r, carry):
                        pass_on(r)
                        return carry

                    lax.fori_loop(1, steps, later, 0)
            lift_cells(s)
            receive(s)
            finish(s, new)
            if half == 0:
                send(s + 1, new)
            else:
                @pl.when(t < steps // 2 - 1)
                def _():
                    send(s + 1, new)
        return carry

    lax.fori_loop(0, steps // 2, pair, 0)

    when_each([
        copy for s in range(steps) for copy in route_x_copies(s) + route_y_copies(s) + row_copies(s) + col_copies(s)
    ], "wait_send")


def write_out(h, m, n, h_hbm, m_hbm, n_hbm, sems):
    copies = [
        pltpu.make_async_copy(src, dst, sems.at[q])
        for q, (src, dst) in enumerate(((h, h_hbm), (m, m_hbm), (n, n_hbm)))
    ]
    for copy in copies:
        copy.start()
    for copy in copies:
        copy.wait()


def shards(n_ox, n_oy, slip_rate, green_kernel, intersection, wet_mask, column_height, east_flow, north_flow):
    steps, faults = slip_rate.shape
    rows, cols = column_height.shape
    up_rows, up_cols = rows // COARSE, cols // COARSE
    part_rows = -(-3 * steps // PAD) * PAD * up_rows
    chunks = 4
    hbm = pl.BlockSpec(memory_space=pltpu.HBM)
    vmem = pl.BlockSpec(memory_space=pltpu.VMEM)
    dma = pltpu.SemaphoreType.DMA
    fields = [jax.ShapeDtypeStruct((rows, cols), f32)] * 3
    result = pl.pallas_call(
        functools.partial(kernel, n_ox, n_oy),
        out_shape=fields,
        in_specs=[vmem, hbm, pl.BlockSpec(memory_space=pltpu.SMEM)] + [hbm] * 4,
        out_specs=[vmem] * 3,
        scratch_shapes=[
            pltpu.VMEM((9, faults, green_kernel.shape[2]), bf16),
            pltpu.VMEM((3, part_rows, up_cols), f32),
        ] + [pltpu.VMEM((rows, cols), f32)] * 3 + [
            pltpu.VMEM((rows, cols), jnp.int32),
            pltpu.VMEM((cols // LANES, rows, LANES), f32),
            pltpu.VMEM((2 * up_cols, cols), bf16),
            pltpu.VMEM((3, rows, LANES), f32),
            pltpu.VMEM((3, LANES, rows), f32),
            pltpu.VMEM((3, rows, LANES), f32),
            pltpu.VMEM((3, part_rows // up_rows, 3 * faults), bf16),
            pltpu.VMEM((steps, 2, 3 * up_rows, up_cols), f32),
            pltpu.VMEM((steps, 3, up_rows, up_cols), f32),
            pltpu.VMEM((steps, 2, up_rows, up_cols), f32),
            pltpu.VMEM((steps, 2, STRIP, cols), f32),
            pltpu.VMEM((steps, 2, STRIP, cols), f32),
            pltpu.VMEM((steps, 2, STRIP, rows), f32),
            pltpu.VMEM((steps, 2, STRIP, rows), f32),
            dma((3, chunks)),
            dma((4,)),
        ] + [dma((steps, 2))] * 8,
        compiler_params=pltpu.CompilerParams(
            collective_id=0, has_side_effects=True, vmem_limit_bytes=52 * 1024 * 1024
        ),
        cost_estimate=pl.CostEstimate(flops=400_000_000, bytes_accessed=16_000_000, transcendentals=0),
    )(slip_rate, green_kernel.transpose(1, 0, 2), intersection, wet_mask, column_height, east_flow, north_flow)
    return pl.pallas_call(
        write_out,
        out_shape=fields,
        in_specs=[vmem] * 3,
        out_specs=[hbm] * 3,
        scratch_shapes=[dma((3,))],
        compiler_params=pltpu.CompilerParams(vmem_limit_bytes=4 * 1024 * 1024),
        cost_estimate=pl.CostEstimate(flops=0, bytes_accessed=6 * rows * cols * 4, transcendentals=0),
    )(*result)


def solution(mesh):
    return jax.shard_map(
        functools.partial(shards, mesh.shape["ox"], mesh.shape["oy"]),
        mesh=mesh,
        in_specs=(
            P(None, ("ox", "oy")),
            P(("ox", "oy"), None, None),
            P(("ox", "oy"), None),
            P("ox", "oy"),
            P("ox", "oy"),
            P("ox", "oy"),
            P("ox", "oy"),
        ),
        out_specs=(P("ox", "oy"), P("ox", "oy"), P("ox", "oy")),
        check_vma=False,
    )
```

```python
import functools

import jax
import jax.numpy as jnp
from jax import lax
from jax.experimental import pallas as pl
from jax.experimental.pallas import tpu as pltpu
from jax.sharding import PartitionSpec as P

COARSE = 4
STRIP = 8
LANES = 128
PAD = 16
GROUP = 8
BLOCK = 32

gravity = 1.0
ratio = 0.2
source = 0.05

MESH = pl.DeviceIdType.MESH
f32 = jnp.float32
bf16 = jnp.bfloat16


def iota(shape, dim):
    return lax.broadcasted_iota(jnp.int32, shape, dim)


def weights(slip_ref, cover_ref, steps, faults, a):
    rows = -(-3 * steps // PAD) * PAD
    wide = 3 * faults
    pick_step = (iota((rows, steps), 0) // 3 == iota((rows, steps), 1)).astype(bf16)
    pick_fault = (iota((faults, wide), 1) % faults == iota((faults, wide), 0)).astype(bf16)
    slips = jnp.dot(pick_step, slip_ref[...], preferred_element_type=f32).astype(bf16)
    slips = jnp.dot(slips, pick_fault, preferred_element_type=f32)
    slot = iota((rows, wide), 0) % 3
    cover = jnp.zeros((rows, wide), f32)
    for b in range(3):
        cover = jnp.where(slot == b, cover_ref[0, 3 * a + b].astype(f32), cover)
    return jnp.where(slot == iota((rows, wide), 1) // faults, slips * cover, 0.0).astype(bf16)


def flux_terms(h, m, n):
    half = 0.5 * ratio
    guess = pl.reciprocal(h, approx=True)
    inv = guess * (2.0 - h * guess)
    u, v = m * inv, n * inv
    east, north = half * m, half * n
    pressure = (0.5 * gravity * half * h) * h
    cross = east * v
    return (0.25 * h, 0.25 * m, 0.25 * n), (east, east * u + pressure, cross), (north, cross, north * v + pressure)


def kernel(
    n_ox, n_oy,
    slip_ref, green_ref, cover_ref, wet_hbm, h_hbm, m_hbm, n_hbm,
    h_out, m_out, n_out,
    green, part, h_0, m_0, n_0, h_1, m_1, n_1, wet, fine, spread, edges, terms, terms_t,
    route_x, summed, route_y, row_out, row_in, col_out, col_in,
    green_sem, load_sem, rx_send, rx_recv, ry_send, ry_recv, row_send, row_recv, col_send, col_recv,
):
    steps, faults = slip_ref.shape
    n_rows, n_cols = wet.shape
    up_rows, up_cols = n_rows // COARSE, n_cols // COARSE
    i, j = lax.axis_index("ox"), lax.axis_index("oy")
    states = ((h_0, m_0, n_0), (h_1, m_1, n_1))
    outs = (h_out, m_out, n_out)
    near = (
        (i > 0, (i - 1, j)),
        (i < n_ox - 1, (i + 1, j)),
        (j > 0, (i, j - 1)),
        (j < n_oy - 1, (i, j + 1)),
    )

    loads = [
        pltpu.make_async_copy(src, dst, load_sem.at[q])
        for q, (src, dst) in enumerate(((h_hbm, h_0), (m_hbm, m_0), (n_hbm, n_0), (wet_hbm, wet)))
    ]
    chunks = green_sem.shape[1]
    width = green.shape[2] // chunks
    greens = {}
    for a in (2, 0, 1):
        for q in range(chunks):
            where = (pl.ds(3 * a, 3), slice(None), pl.ds(q * width, width))
            greens[a, q] = pltpu.make_async_copy(green_ref.at[where], green.at[where], green_sem.at[a, q])
            greens[a, q].start()
        if a == 2:
            for copy in loads:
                copy.start()

    barrier = pltpu.get_barrier_semaphore()
    for there, device in near:
        @pl.when(there)
        def _():
            pl.semaphore_signal(barrier, inc=1, device_id=device, device_id_type=MESH)

    zero_x = jnp.zeros(route_x.shape[2:], f32)
    zero_y = jnp.zeros(route_y.shape[2:], f32)
    for d in range(2):
        @pl.when(jnp.logical_not(near[d][0]))
        def _():
            for s in range(steps):
                route_x[s, d] = zero_x

        @pl.when(jnp.logical_not(near[2 + d][0]))
        def _():
            for s in range(steps):
                route_y[s, d] = zero_y

    coarse_of = iota((2 * up_cols, n_cols), 1) // COARSE
    spread[...] = (coarse_of == iota((2 * up_cols, n_cols), 0) % up_cols).astype(bf16)
    terms[...] = jnp.zeros(terms.shape, f32)
    row_out[...] = jnp.zeros(row_out.shape, f32)
    col_out[...] = jnp.zeros(col_out.shape, f32)
    lhs = [weights(slip_ref, cover_ref, steps, faults, a) for a in range(3)]

    pl.semaphore_wait(barrier, sum(there.astype(jnp.int32) for there, _ in near))

    def remote(src, dst, send, recv, d):
        return pltpu.make_async_remote_copy(
            src_ref=src, dst_ref=dst, send_sem=send, recv_sem=recv, device_id=near[d][1], device_id_type=MESH
        )

    def when_each(copies, what):
        for d, copy in copies:
            @pl.when(near[d ^ 1 if what == "wait_recv" else d][0])
            def _():
                getattr(copy, what)()

    def route_x_copies(s, sides=(0, 1)):
        rows = 3 * up_rows
        return [
            (d, remote(part.at[2 * d, pl.ds(s * rows, rows)], route_x.at[s, 1 - d], rx_send.at[s, d], rx_recv.at[s, 1 - d], d))
            for d in sides
        ]

    def route_y_copies(s):
        return [
            (2 + d, remote(summed.at[s, d], route_y.at[s, 1 - d], ry_send.at[s, d], ry_recv.at[s, 1 - d], 2 + d))
            for d in range(2)
        ]

    def row_copies(s):
        return [(d, remote(row_out.at[s, d], row_in.at[s, 1 - d], row_send.at[s, d], row_recv.at[s, 1 - d], d)) for d in range(2)]

    def col_copies(s):
        return [
            (2 + d, remote(col_out.at[s, d], col_in.at[s, 1 - d], col_send.at[s, d], col_recv.at[s, 1 - d], 2 + d))
            for d in range(2)
        ]

    first_block = pl.ds(0, LANES)
    last_block = pl.ds(n_cols - LANES, LANES)
    n_strips = n_rows // STRIP
    row8 = iota((STRIP, n_cols), 0)
    lane8 = iota((STRIP, LANES), 1)
    lane = iota((BLOCK, LANES), 1)

    def send_edges(s):
        for c in range(3):
            turned = jnp.transpose(edges[c])
            col_out[s, 0, pl.ds(c, 1)] = turned[:1]
            col_out[s, 1, pl.ds(c, 1)] = turned[LANES - 1:]
        when_each(col_copies(s), "start")

    def send_rows(s, state):
        for c in range(3):
            row_out[s, 0, pl.ds(c, 1)] = state[c][pl.ds(0, 1)]
            row_out[s, 1, pl.ds(c, 1)] = state[c][pl.ds(n_rows - 1, 1)]
        when_each(row_copies(s), "start")

    def matmul(a):
        for q in range(chunks):
            greens[a, q].wait()
            block = green[pl.ds(3 * a, 3), :, pl.ds(q * width, width)].reshape(3 * faults, width)
            out = jnp.dot(lhs[a], block, preferred_element_type=f32)
            for p in range(width // up_cols):
                row = q * (width // up_cols) + p
                part[a, pl.ds(row, out.shape[0], stride=up_rows), :] = out[:, p * up_cols:(p + 1) * up_cols]

    def pass_on(s):
        when_each(route_x_copies(s), "wait_recv")
        mine = part[1, pl.ds(s * 3 * up_rows, 3 * up_rows), :]
        total = mine + route_x[s, 0] + route_x[s, 1]
        summed[s, 0] = total[:up_rows]
        summed[s, 1] = total[2 * up_rows:]
        summed[s, 2] = total[up_rows:2 * up_rows]
        when_each(route_y_copies(s), "start")

    def lift_cells(s):
        when_each(route_y_copies(s), "wait_recv")
        lift = source * (summed[s, 2] + route_y[s, 0] + route_y[s, 1])
        high = lift.astype(bf16)
        low = (lift - high.astype(f32)).astype(bf16)
        wide = jnp.dot(jnp.concatenate([high, low], axis=1), spread[...], preferred_element_type=f32)
        for b in range(n_cols // LANES):
            for t in range(COARSE):
                fine[b, pl.ds(t, up_rows, stride=COARSE), :] = wide[:, b * LANES:(b + 1) * LANES]

    def beside(plus, minus):
        n_blocks = n_cols // LANES
        blocks = [slice(b * LANES, (b + 1) * LANES) for b in range(n_blocks)]
        after = [pltpu.roll(plus[:, block], LANES - 1, 1) for block in blocks] + [0.0]
        before = [0.0] + [pltpu.roll(minus[:, block], 1, 1) for block in blocks]
        return jnp.concatenate([
            jnp.where(lane8 == LANES - 1, after[b + 1], after[b]) + jnp.where(lane8 == 0, before[b], before[b + 1])
            for b in range(n_blocks)
        ], axis=1)

    def bulk(state, new):
        def start(base, down_before):
            quarter, fx, fy = flux_terms(*(field[pl.ds(base, STRIP)] for field in state))
            up = [pltpu.roll(quarter[c] - fx[c], STRIP - 1, 0) for c in range(3)]
            down = [pltpu.roll(quarter[c] + fx[c], 1, 0) for c in range(3)]
            sides = [beside(quarter[c] - fy[c], quarter[c] + fy[c]) for c in range(3)]
            acc = [sides[c] + jnp.where(row8 == 0, down_before[c], down[c]) for c in range(3)]
            return acc, up, down

        def store(base, acc, up, next_up):
            dry = wet[pl.ds(base, STRIP)].astype(f32)
            for c in range(3):
                value = acc[c] + jnp.where(row8 == STRIP - 1, next_up[c], up[c])
                new[c][pl.ds(base, STRIP)] = value * dry if c > 0 else value

        def group(base, carry):
            for u in range(GROUP):
                now = start(base + u * STRIP, carry[2])
                if carry[0] is not None:
                    store(base + (u - 1) * STRIP, carry[0], carry[1], now[1])
                carry = now
            return carry

        zero = jnp.zeros((STRIP, n_cols), f32)
        carry = group(0, (None, None, [zero] * 3))
        carry = lax.fori_loop(
            1, n_strips // GROUP, lambda t, carry: group(pl.multiple_of(t * GROUP * STRIP, GROUP * STRIP), carry), carry
        )
        store(n_rows - STRIP, carry[0], carry[1], [zero] * 3)

    def receive(s):
        when_each(row_copies(s), "wait_recv")
        when_each(col_copies(s), "wait_recv")
        for d in range(2):
            @pl.when(jnp.logical_not(near[d][0]))
            def _():
                row_in[s, d] = row_out[s, d]

            @pl.when(jnp.logical_not(near[2 + d][0]))
            def _():
                col_in[s, d] = col_out[s, d]

        for d in range(2):
            quarter, _, fy = flux_terms(*(col_in[s, d, pl.ds(c, 1)] for c in range(3)))
            for c in range(3):
                terms[c, pl.ds(d * (LANES - 1), 1)] = quarter[c] - fy[c] if d else quarter[c] + fy[c]
        for c in range(3):
            terms_t[c] = jnp.transpose(terms[c])

    def finish(s, new):
        for d in range(2):
            row = pl.ds(d * (n_rows - 1), 1)
            quarter, fx, _ = flux_terms(*(row_in[s, d, pl.ds(c, 1)] for c in range(3)))
            dry = wet[row].astype(f32)
            for c in range(3):
                term = quarter[c] - fx[c] if d else quarter[c] + fx[c]
                new[c][row] = new[c][row] + (term * dry if c > 0 else term)

        def body(t, carry):
            where = pl.ds(pl.multiple_of(t * BLOCK, BLOCK), BLOCK)
            dry_first = wet[where, first_block].astype(f32)
            dry_last = wet[where, last_block].astype(f32)
            for b in range(n_cols // LANES):
                block = pl.ds(b * LANES, LANES)
                new[0][where, block] = new[0][where, block] + fine[b, where]
            for c in range(3):
                term = terms_t[c, where]
                left = jnp.where(lane == 0, term, 0.0)
                right = jnp.where(lane == LANES - 1, term, 0.0)
                first = new[c][where, first_block] + (left * dry_first if c > 0 else left)
                last = new[c][where, last_block] + (right * dry_last if c > 0 else right)
                new[c][where, first_block] = first
                new[c][where, last_block] = last
                if s < steps - 1:
                    edges[c, where] = jnp.where(lane == 0, first, last)
            return carry

        lax.fori_loop(0, n_rows // BLOCK, body, 0)

    matmul(2)
    for copy in loads:
        copy.wait()
    for c in range(3):
        edges[c] = jnp.where(iota((n_rows, LANES), 1) == 0, states[0][c][:, first_block], states[0][c][:, last_block])
    send_rows(0, states[0])
    send_edges(0)
    when_each(route_x_copies(0, (1,)), "start")
    matmul(0)
    when_each(route_x_copies(0, (0,)), "start")
    when_each(route_x_copies(1), "start")
    matmul(1)
    pass_on(0)
    for s in range(steps):
        state = states[s % 2]
        new = outs if s == steps - 1 else states[1 - s % 2]
        bulk(state, new)
        if s + 1 < steps:
            pass_on(s + 1)
        if s + 2 < steps:
            when_each(route_x_copies(s + 2), "start")
        lift_cells(s)
        receive(s)
        finish(s, new)
        if s < steps - 1:
            send_rows(s + 1, new)
            send_edges(s + 1)

    for s in range(steps):
        when_each(route_x_copies(s), "wait_send")
        when_each(route_y_copies(s), "wait_send")
        when_each(row_copies(s), "wait_send")
        when_each(col_copies(s), "wait_send")


def write_out(h, m, n, h_hbm, m_hbm, n_hbm, sems):
    copies = [
        pltpu.make_async_copy(src, dst, sems.at[q])
        for q, (src, dst) in enumerate(((h, h_hbm), (m, m_hbm), (n, n_hbm)))
    ]
    for copy in copies:
        copy.start()
    for copy in copies:
        copy.wait()


def shards(n_ox, n_oy, slip_rate, green_kernel, intersection, wet_mask, column_height, east_flow, north_flow):
    steps, faults = slip_rate.shape
    rows, cols = column_height.shape
    up_rows, up_cols = rows // COARSE, cols // COARSE
    part_rows = -(-3 * steps // PAD) * PAD * up_rows
    chunks = 4
    hbm = pl.BlockSpec(memory_space=pltpu.HBM)
    vmem = pl.BlockSpec(memory_space=pltpu.VMEM)
    dma = pltpu.SemaphoreType.DMA
    fields = [jax.ShapeDtypeStruct((rows, cols), f32)] * 3
    result = pl.pallas_call(
        functools.partial(kernel, n_ox, n_oy),
        out_shape=fields,
        in_specs=[vmem, hbm, pl.BlockSpec(memory_space=pltpu.SMEM)] + [hbm] * 4,
        out_specs=[vmem] * 3,
        scratch_shapes=[
            pltpu.VMEM((9, faults, green_kernel.shape[2]), bf16),
            pltpu.VMEM((3, part_rows, up_cols), f32),
        ] + [pltpu.VMEM((rows, cols), f32)] * 6 + [
            pltpu.VMEM((rows, cols), jnp.int32),
            pltpu.VMEM((cols // LANES, rows, LANES), f32),
            pltpu.VMEM((2 * up_cols, cols), bf16),
            pltpu.VMEM((3, rows, LANES), f32),
            pltpu.VMEM((3, LANES, rows), f32),
            pltpu.VMEM((3, rows, LANES), f32),
            pltpu.VMEM((steps, 2, 3 * up_rows, up_cols), f32),
            pltpu.VMEM((steps, 3, up_rows, up_cols), f32),
            pltpu.VMEM((steps, 2, up_rows, up_cols), f32),
            pltpu.VMEM((steps, 2, STRIP, cols), f32),
            pltpu.VMEM((steps, 2, STRIP, cols), f32),
            pltpu.VMEM((steps, 2, STRIP, rows), f32),
            pltpu.VMEM((steps, 2, STRIP, rows), f32),
            dma((3, chunks)),
            dma((4,)),
        ] + [dma((steps, 2))] * 8,
        compiler_params=pltpu.CompilerParams(
            collective_id=0, has_side_effects=True, vmem_limit_bytes=52 * 1024 * 1024
        ),
        cost_estimate=pl.CostEstimate(flops=400_000_000, bytes_accessed=16_000_000, transcendentals=0),
    )(slip_rate, green_kernel.transpose(1, 0, 2), intersection, wet_mask, column_height, east_flow, north_flow)
    return pl.pallas_call(
        write_out,
        out_shape=fields,
        in_specs=[vmem] * 3,
        out_specs=[hbm] * 3,
        scratch_shapes=[dma((3,))],
        compiler_params=pltpu.CompilerParams(vmem_limit_bytes=4 * 1024 * 1024),
        cost_estimate=pl.CostEstimate(flops=0, bytes_accessed=6 * rows * cols * 4, transcendentals=0),
    )(*result)


def solution(mesh):
    return jax.shard_map(
        functools.partial(shards, mesh.shape["ox"], mesh.shape["oy"]),
        mesh=mesh,
        in_specs=(
            P(None, ("ox", "oy")),
            P(("ox", "oy"), None, None),
            P(("ox", "oy"), None),
            P("ox", "oy"),
            P("ox", "oy"),
            P("ox", "oy"),
            P("ox", "oy"),
        ),
        out_specs=(P("ox", "oy"), P("ox", "oy"), P("ox", "oy")),
        check_vma=False,
    )
```
